128 devices in a mesh: slab: 64 (over x, z_hi, y, core), batch: 2 (over z_lo).
Axes of the slice: x: 4, y: 4, z: 4 (z_hi: 2, z_lo: 2; z = z_hi * 2 + z_lo), core: 2. Of those that a mesh axis runs over, the one named last changes fastest.
Arguments:
- field: bfloat16 [2, 16, 512, 256, 128], P('batch', None, 'slab'), may hold values from -6 to 6
- cotangent: bfloat16 [2, 16, 512, 256, 128], P('batch', None, 'slab'), may hold values from -6 to 6
- spectral_weight: bfloat16 [1024, 2, 16, 512], P('slab'), may hold values from -1 to 1
- point_weight: bfloat16 [16, 16], replicated, may hold values from -1.5 to 1.5
- point_bias: float32 [16], replicated, may hold values from -3 to 3
Outputs:
- input_grad: bfloat16 [2, 16, 512, 256, 128], P('batch', None, 'slab')
- grad_spec: float32 [1024, 2, 16, 512], P('slab')
- grad_point: float32 [16, 16], replicated
- grad_bias: float32 [16], replicated
The draws below stay inside these ranges and needn't reach their ends.
All inputs are finite; a program needn't handle non-finite values.
Results may differ from the reference program's by a relative error of at most 0.018.
Values may be sent and summed in bfloat16 or wider, within the bound.
No kernel may reach another device: no remote copies, remote signals or barrier semaphores. Data moves between devices by JAX's collectives and lax.ppermute only.
A program may use at most 192 MiB of HBM per device.

```python
import math
import jax
import jax.numpy as jnp
from jax import lax

C = 16
MX = 32
MY = 32
MZ = 32
NY = 256
NZ = 128
CX = 8
NX = 512
PAIRS = 1024
SAMPLES = 2
N_SLAB = 64


def level_of(rng, extent, pieces, least, high):
    def one(dim, parts):
        draws = jax.random.uniform(jax.random.fold_in(jax.random.fold_in(rng, 6), dim), (parts,), jnp.float32, least / len(pieces), high / len(pieces))
        return jnp.repeat(jnp.exp(draws), extent[dim] // parts).reshape((-1,) + (1,) * (len(extent) - dim - 1))

    factor_of = one(*pieces[0])
    for cut in pieces[1:]:
        factor_of = factor_of * one(*cut)
    return factor_of


def gaussian(rng, shape, spread, bound, cuts=(), kind=jnp.bfloat16):
    values = jax.random.normal(rng, shape, jnp.float32) * spread
    if len(cuts) > 0:
        values = level_of(rng, shape, cuts, -0.22, 0.18) * values
    return jnp.clip(values, min=-bound, max=bound).astype(kind)


def setup_inputs(seed: int = 0) -> dict:
    keys = jax.random.split(jax.random.key(seed), 6)
    return {
        "field": gaussian(keys[0], (SAMPLES, C, NX, NY, NZ), 1.0, 6.0, ((0, 2), (2, 64))),
        "cotangent": gaussian(keys[1], (SAMPLES, C, NX, NY, NZ), 1.0, 6.0, ((0, 2), (2, 64))),
        "spectral_weight": gaussian(keys[2], (PAIRS, 2, C, C * MX), (2 * C) ** -0.5, 1.0, ((0, 64),)),
        "point_weight": gaussian(keys[3], (C, C), C ** -0.5, 1.5),
        "point_bias": gaussian(keys[4], (C,), 0.5, 3.0, (), jnp.float32),
    }


def float_einsum(form, left, right):
    return jnp.einsum(form, left.astype(jnp.float32), right.astype(jnp.float32), precision=lax.Precision.HIGHEST)

def mode_freqs(number, length):
    indices = jnp.arange(number, dtype=jnp.int32)
    return jnp.where(indices < number // 2, indices, indices + (length - number))

def phase_grid(positions, frequencies, length):
    product = positions[:, None] * frequencies[None, :] % length
    return product.astype(jnp.float32) * (2.0 * math.pi / length)

def rotation(phases, orient):
    cosine = jnp.cos(phases)
    sine_part = orient * jnp.sin(phases)
    upper = jnp.stack([cosine, -sine_part], axis=1)
    lower = jnp.stack([sine_part, cosine], axis=1)
    return jnp.stack([upper, lower], axis=0).astype(jnp.bfloat16)

def plane_tables(rows_y, rows_z):
    phase_y = phase_grid(jnp.arange(rows_y, dtype=jnp.int32), mode_freqs(MY, rows_y), rows_y)
    phase_z = phase_grid(jnp.arange(rows_z, dtype=jnp.int32), jnp.arange(MZ, dtype=jnp.int32), rows_z)
    forward_y = jnp.stack([jnp.cos(phase_y), -jnp.sin(phase_y)], axis=1).astype(jnp.bfloat16)
    forward_z = rotation(phase_z, 1.0)
    inverse_z = rotation(phase_z.T, -1.0)
    inverse_y = jnp.stack([jnp.cos(phase_y).T, -jnp.sin(phase_y).T], axis=0).astype(jnp.bfloat16)
    return (forward_y, forward_z, inverse_z, inverse_y)

def yz_forward(slab_data, tables):
    partial_value = float_einsum('bcxyz,yrm->bcxrmz', slab_data, tables[0]).astype(jnp.bfloat16)
    spectrum = float_einsum('bcxrmz,rzsk->bcxsmk', partial_value, tables[1]).astype(jnp.bfloat16)
    return spectrum.reshape(spectrum.shape[:4] + (MY * MZ,))

def yz_inverse(planes_in, tables, factor):
    shaped = planes_in.reshape(planes_in.shape[:4] + (MY, MZ))
    rolled = float_einsum('boxsmk,skrz->boxrmz', shaped, tables[2]).astype(jnp.bfloat16)
    return factor * float_einsum('boxrmz,rmy->boxyz', rolled, tables[3])

def x_forward(spectrum, table, factor):
    return factor * float_einsum('bcxrp,rxsa->bcsap', spectrum, table)

def x_inverse(spectrum, table):
    return float_einsum('bosap,sarx->boxrp', spectrum, table).astype(jnp.bfloat16)

def mix_modes(spectrum, weights_f):

    def apply(values, weight_part):
        return jnp.einsum('biap,pioa->boap', values, weight_part, precision=lax.Precision.HIGHEST)
    real_part, imag_part = (spectrum[:, :, 0], spectrum[:, :, 1])
    first = apply(real_part, weights_f[:, 0]) - apply(imag_part, weights_f[:, 1])
    second = apply(real_part, weights_f[:, 1]) + apply(imag_part, weights_f[:, 0])
    return jnp.stack([first, second], axis=2)

def adjoint_mix(spectrum, weights_f):

    def apply(values, weight_part):
        return jnp.einsum('boap,pioa->biap', values, weight_part, precision=lax.Precision.HIGHEST)
    real_part, imag_part = (spectrum[:, :, 0], spectrum[:, :, 1])
    first = apply(real_part, weights_f[:, 0]) + apply(imag_part, weights_f[:, 1])
    second = apply(imag_part, weights_f[:, 0]) - apply(real_part, weights_f[:, 1])
    return jnp.stack([first, second], axis=2)

def weight_grad(modes_in, modes_out):

    def apply(left, right):
        return jnp.einsum('biap,boap->pioa', left, right, precision=lax.Precision.HIGHEST)
    first = apply(modes_in[:, :, 0], modes_out[:, :, 0]) + apply(modes_in[:, :, 1], modes_out[:, :, 1])
    second = apply(modes_in[:, :, 0], modes_out[:, :, 1]) - apply(modes_in[:, :, 1], modes_out[:, :, 0])
    stacked = jnp.stack([first, second], axis=1)
    return stacked.reshape(stacked.shape[0], 2, stacked.shape[2], stacked.shape[3] * stacked.shape[4])

def activation_grad(pre, upstream):
    _, pull = jax.vjp(lambda values: jax.nn.gelu(values, approximate=True), pre)
    return pull(upstream)[0]

def split_blocks(array):
    shaped = array.reshape((array.shape[0], array.shape[1], N_SLAB, CX) + array.shape[3:])
    return jnp.moveaxis(shaped, 2, 0)

def join_blocks(array):
    moved = jnp.moveaxis(array, 0, 2)
    return moved.reshape((moved.shape[0], moved.shape[1], N_SLAB * CX) + moved.shape[4:])

def reference(field, cotangent, spectral_weight, point_weight, point_bias):
    tables = plane_tables(NY, NZ)
    phase_x = phase_grid(jnp.arange(NX, dtype=jnp.int32), mode_freqs(MX, NX), NX)
    forward_x = rotation(phase_x, 1.0)
    inverse_x = rotation(phase_x.T, -1.0)
    scale_f = 1.0 / math.sqrt(NX * NY * NZ)
    scale_i = 1.0 / math.sqrt(MX * MY * MZ)
    scale_p = 1.0 / math.sqrt(SAMPLES * NX * NY * NZ)
    scale_w = math.sqrt(MX * MY * MZ / (SAMPLES * NX * NY * NZ))
    weights_f = spectral_weight.astype(jnp.float32).reshape(PAIRS, 2, C, C, MX)
    field_blocks = split_blocks(field)
    cot_blocks = split_blocks(cotangent)
    planes_u = join_blocks(lax.map(lambda slab_data: yz_forward(slab_data, tables), field_blocks))
    modes_u = x_forward(planes_u, forward_x, scale_f)
    mixed = mix_modes(modes_u, weights_f).astype(jnp.bfloat16)
    back_v = split_blocks(x_inverse(mixed, inverse_x))

    def signal(field_part, cot_part, back_part):
        pre = yz_inverse(back_part, tables, scale_i) + float_einsum('bixyz,io->boxyz', field_part, point_weight)
        pre = pre + point_bias[None, :, None, None, None]
        return activation_grad(pre, cot_part.astype(jnp.float32)).astype(jnp.bfloat16)

    def first_pass(inputs):
        dpre = signal(inputs[0], inputs[1], inputs[2])
        point_part = float_einsum('bixyz,boxyz->io', inputs[0], dpre)
        bias_part = lax.optimization_barrier(jnp.sum(dpre.astype(jnp.float32), axis=(0, 2, 3, 4)))
        return (yz_forward(dpre, tables), point_part, bias_part)
    spec_blocks, point_parts, bias_parts = lax.map(first_pass, (field_blocks, cot_blocks, back_v))
    grad_point = scale_p * lax.optimization_barrier(jnp.sum(point_parts, axis=0))
    grad_bias = scale_p * lax.optimization_barrier(jnp.sum(bias_parts, axis=0))
    modes_d = x_forward(join_blocks(spec_blocks), forward_x, scale_i)
    grad_spec = scale_w * weight_grad(modes_u, modes_d)
    back_d = split_blocks(x_inverse(adjoint_mix(modes_d, weights_f).astype(jnp.bfloat16), inverse_x))

    def second_pass(inputs):
        dpre = signal(inputs[0], inputs[1], inputs[2])
        total = yz_inverse(inputs[3], tables, scale_f) + float_einsum('boxyz,io->bixyz', dpre, point_weight)
        return total.astype(jnp.bfloat16)
    input_grad = join_blocks(lax.map(second_pass, (field_blocks, cot_blocks, back_v, back_d)))
    return (input_grad, grad_spec, grad_point, grad_bias)
```

```python
import math

import jax
import jax.numpy as jnp
import numpy as np
from jax import lax
from jax.experimental import pallas as pl
from jax.experimental.pallas import tpu as pltpu
from jax.sharding import PartitionSpec as P

C = 16
X = 8
NY = 256
NZ = 128
NX = 512
MODES = 32
SLABS = 64
CELLS = NX * NY * NZ
SCALE_F = 1.0 / math.sqrt(CELLS)
SCALE_I = 1.0 / math.sqrt(MODES**3)
SCALE_P = 1.0 / math.sqrt(2 * CELLS)
SCALE_W = math.sqrt(MODES**3 / (2 * CELLS))
GELU_A = math.sqrt(2.0 / math.pi)
GK = (GELU_A * 0.044715) ** (1.0 / 3.0)
GA = GELU_A / GK
BOTH = ("slab", "batch")
F32 = jnp.float32
BF16 = jnp.bfloat16
MIB = 1 << 20


def freqs(number, length):
    index = np.arange(number)
    return np.where(index < number // 2, index, index + length - number)


def angles(length, frequencies):
    product = (np.arange(length)[:, None] * frequencies[None, :]) % length
    return product * (2.0 * math.pi / length)


def tables():
    thy = angles(NY, freqs(MODES, NY))
    thz = angles(NZ, np.arange(MODES))
    thx = angles(NX, freqs(MODES, NX))
    ty = np.concatenate([np.cos(thy).T, -np.sin(thy).T], axis=0)
    cos, sin = np.cos(thz), np.sin(thz)
    rot = np.zeros((2, NZ, 2, MODES))
    rot[0, :, 0], rot[1, :, 0] = cos, sin
    rot[1, :, 1], rot[0, :, 1] = cos, -sin
    zb = rot.reshape(2, NZ, 2, 4, 8).transpose(0, 1, 3, 2, 4)[:, :, :, :, None, :]
    zb = np.broadcast_to(zb, (2, NZ, 4, 2, 8, 8)).reshape(2 * NZ, 512)
    cs = np.stack([np.cos(thx), np.sin(thx)]).reshape(2, SLABS, X, MODES)
    tx = np.zeros((2, 2, 4, MODES, SLABS, 2, X))
    txi = np.zeros((SLABS, 2, X, 2, 2, MODES))
    for half in range(2):
        tx[half, :, :, :, :, half] = cs.transpose(0, 3, 1, 2)[:, None]
        txi[:, half, :, half] = cs.transpose(1, 2, 0, 3)
    return tuple(
        np.asarray(t, np.float32).astype(BF16)
        for t in (ty, ty.T, zb, tx.reshape(512, 1024), txi.reshape(1024, 128))
    )


def dot(left, right):
    return jnp.dot(left, right, preferred_element_type=F32)


def dot_nt(left, right):
    return lax.dot_general(left, right, (((1,), (1,)), ((), ())), preferred_element_type=F32)


def build_z(zb_ref, zf_ref):
    table = zb_ref[...].astype(F32)
    channel = (lax.broadcasted_iota(jnp.int32, (2 * NZ, 512), 1) // 8) % 8
    for c in range(8):
        zf_ref[c * 256 : (c + 1) * 256, :] = jnp.where(channel == c, table, 0.0).astype(BF16)


def z_forward(planes_ref, zf_ref, wide_ref, out_ref):
    for half in range(2):
        result = dot(planes_ref[half * 256 : (half + 1) * 256, :], zf_ref[...])
        for x in range(X):
            for kq in range(4):
                wide_ref[pl.ds(kq * 16 + half * 8 + x, 32, stride=64), :] = result[
                    x * 32 : (x + 1) * 32, kq * 128 : (kq + 1) * 128
                ]
    out_ref[...] = wide_ref[...].astype(BF16).reshape(128, 16, 128)


def z_inverse(in_ref, zf_ref, wide_ref, gather_ref, rolled_ref):
    wide_ref[...] = in_ref[...].astype(F32).reshape(2048, 128)
    for half in range(2):
        for x in range(X):
            for kq in range(4):
                row = (half * 8 + x) * 32
                gather_ref[row : row + 32, kq * 128 : (kq + 1) * 128] = wide_ref[
                    pl.ds(kq * 16 + half * 8 + x, 32, stride=64), :
                ].astype(BF16)
    for c in range(8):
        rolled_ref[:, c * 256 : (c + 1) * 256] = dot_nt(
            gather_ref[...], zf_ref[c * 256 : (c + 1) * 256, :]
        ).astype(BF16)


def y_forward(ty_ref, pair, planes_ref, x, op):
    result = dot(ty_ref[...], pair)
    half, first = op // 4, (op % 4) * 2
    rows = pl.ds(pl.multiple_of(half * 256 + x * 32, 32), 32)
    for j in range(2):
        for part in range(2):
            column = (first + j) * 256 + part * 128
            planes_ref[rows, column : column + 128] = result[
                part * 32 : (part + 1) * 32, j * 128 : (j + 1) * 128
            ].astype(BF16)
    return result


def y_inverse(tyt_ref, rolled_ref, x, op):
    half, first = op // 4, (op % 4) * 2
    rows = pl.ds(pl.multiple_of(half * 256 + x * 32, 32), 32)
    blocks = []
    for j in range(2):
        column = (first + j) * 256
        blocks.append(
            jnp.concatenate(
                [
                    rolled_ref[rows, column : column + 128],
                    rolled_ref[rows, column + 128 : column + 256],
                ],
                axis=0,
            )
        )
    return dot(tyt_ref[...], jnp.concatenate(blocks, axis=1))


def field_kernel(field_ref, ty_ref, zb_ref, out_ref, zf_ref, planes_ref, wide_ref):
    x = pl.program_id(0)

    @pl.when(x == 0)
    def _():
        build_z(zb_ref, zf_ref)

    for op in range(8):
        pair = jnp.concatenate([field_ref[2 * op], field_ref[2 * op + 1]], axis=1)
        y_forward(ty_ref, pair, planes_ref, x, op)

    @pl.when(x == X - 1)
    def _():
        z_forward(planes_ref, zf_ref, wide_ref, out_ref)


def y_blocks(ref):
    return jnp.concatenate(
        [ref[:, b * 16 : (b + 1) * 16, :].reshape(256, 128) for b in range(16)], axis=1
    )


def map_kernel(scale, in_ref, kron_ref, bias_ref, out_ref):
    for b in range(8):
        pair = jnp.concatenate(
            [in_ref[:, y : y + 16, :].reshape(256, 128) for y in (b * 32, b * 32 + 16)], axis=1
        )
        result = dot(kron_ref[...], pair)
        if bias_ref is not None:
            result = result + bias_ref[...]
        result = (result * scale).astype(BF16)
        for j in range(2):
            y = b * 32 + j * 16
            out_ref[:, y : y + 16, :] = result[:, j * 128 : (j + 1) * 128].reshape(C, 16, 128)


def pre_kernel(in_ref, kron_ref, bias_ref, out_ref):
    map_kernel(GK, in_ref, kron_ref, bias_ref, out_ref)


def back_kernel(in_ref, kron_ref, out_ref):
    map_kernel(0.5, in_ref, kron_ref, None, out_ref)


def signal_kernel(
    in_ref, pre_ref, cot_ref, ty_ref, tyt_ref, zb_ref,
    dpre_ref, out_ref, bias_ref,
    zf_ref, planes_ref, wide_ref, gather_ref, rolled_ref,
):
    x = pl.program_id(0)

    @pl.when(x == 0)
    def _():
        build_z(zb_ref, zf_ref)
        z_inverse(in_ref, zf_ref, wide_ref, gather_ref, rolled_ref)
        bias_ref[...] = jnp.zeros_like(bias_ref)

    for op in range(8):
        back = y_inverse(tyt_ref, rolled_ref, x, op)
        pair = []
        for j in range(2):
            o = 2 * op + j
            h = back[:, j * 128 : (j + 1) * 128] + pre_ref[o].astype(F32)
            square = h * h
            t = jnp.tanh(h * (square + GA))
            slope = h * (square * 3.0 + GA)
            d = (1.0 + t) * (1.0 + (1.0 - t) * slope) * cot_ref[o].astype(F32)
            d = d.astype(BF16)
            dpre_ref[o] = d
            pair.append(d)
        result = y_forward(ty_ref, jnp.concatenate(pair, axis=1), planes_ref, x, op)
        bias_ref[op : op + 1, :] += result[0:1, :]

    @pl.when(x == X - 1)
    def _():
        z_forward(planes_ref, zf_ref, wide_ref, out_ref)


def final_kernel(
    in_ref, mapped_ref, tyt_ref, zb_ref, out_ref, zf_ref, wide_ref, gather_ref, rolled_ref
):
    x = pl.program_id(0)

    @pl.when(x == 0)
    def _():
        build_z(zb_ref, zf_ref)
        z_inverse(in_ref, zf_ref, wide_ref, gather_ref, rolled_ref)

    for op in range(8):
        back = y_inverse(tyt_ref, rolled_ref, x, op)
        for j in range(2):
            o = 2 * op + j
            out_ref[o] = (back[:, j * 128 : (j + 1) * 128] + mapped_ref[o].astype(F32)).astype(BF16)


def x_forward(in_ref, tx_ref, scale, modes_ref):
    data = jnp.concatenate([in_ref[:, b].reshape(1024, 128) for b in range(2)], axis=1)
    raw = dot(tx_ref[...], data)
    lane = lax.broadcasted_iota(jnp.int32, (128, 128), 1)
    sign = jnp.where(lane < 64, scale, -scale)
    for half in range(2):
        for b in range(2):
            cosine = raw[half * 256 : half * 256 + 128, b * 128 : (b + 1) * 128]
            sine = raw[half * 256 + 128 : half * 256 + 256, b * 128 : (b + 1) * 128]
            modes = cosine * scale + pltpu.roll(sine, 64, 1) * sign
            row = (half * 2 + b) * 128
            modes_ref[row : row + 128, :] = modes.T


def x_inverse(mixed, txi_ref, out_ref):
    lane = lax.broadcasted_iota(jnp.int32, (32, 128), 1)
    rows = []
    for half in range(2):
        turned = [mixed(half, b).T[:32] for b in range(2)]
        rows.append(jnp.concatenate(turned, axis=1))
        rows.append(
            jnp.concatenate(
                [jnp.where(lane < 64, -1.0, 1.0) * pltpu.roll(g, 64, 1) for g in turned], axis=1
            )
        )
    result = dot(txi_ref[...], jnp.concatenate(rows, axis=0).astype(BF16)).astype(BF16)
    for b in range(2):
        out_ref[:, b] = result[:, b * 128 : (b + 1) * 128].reshape(SLABS, 16, 128)


def mix_kernel(which_ref, in_ref, weight_ref, tx_ref, txi_ref, out_ref, modes_ref, mixed_ref):
    x_forward(in_ref, tx_ref, SCALE_F, modes_ref)
    first = which_ref[0] * 8
    for p in range(8):
        real = weight_ref[first + p, 0].astype(F32)
        imag = weight_ref[first + p, 1].astype(F32)
        for b in range(2):
            u = [
                [modes_ref[pl.ds((half * 2 + b) * 128 + s * 64 + p, 8, stride=8), :] for s in range(2)]
                for half in range(2)
            ]
            for q in range(4):
                total = [0.0, 0.0]
                for half in range(2):
                    w0 = real[half * 8 : half * 8 + 8, q * 128 : (q + 1) * 128]
                    w1 = imag[half * 8 : half * 8 + 8, q * 128 : (q + 1) * 128]
                    u0, u1 = u[half]
                    total[0] = total[0] + (u0 * w0 - u1 * w1)
                    total[1] = total[1] + (u0 * w1 + u1 * w0)
                for s in range(2):
                    row = (b * 2 + s) * 8 + p
                    mixed_ref[row : row + 1, q * 128 : (q + 1) * 128] = jnp.sum(
                        total[s], axis=0, keepdims=True
                    ) * (SCALE_I * GK)

    def mixed(half, b):
        pieces = []
        for s in range(2):
            row = (b * 2 + s) * 8
            for c in range(8):
                q, r = divmod(half * 8 + c, 4)
                piece = mixed_ref[row : row + 8, q * 128 : (q + 1) * 128]
                pieces.append(pltpu.roll(piece, (128 - 32 * r) % 128, 1) if r else piece)
        return jnp.concatenate(pieces, axis=0)

    x_inverse(mixed, txi_ref, out_ref)


def adjoint_kernel(
    which_ref, in_ref, weight_ref, tx_ref, txi_ref, out_ref, rows_ref, modes_ref, mixed_ref
):
    x_forward(in_ref, tx_ref, 0.5 * SCALE_I, modes_ref)
    group = lax.broadcasted_iota(jnp.int32, (8, 128), 1) // 32
    for b in range(2):
        for s in range(2):
            for q in range(4):
                half, c = q // 2, (q % 2) * 4
                row = (half * 2 + b) * 128 + s * 64 + c * 8
                value = modes_ref[row : row + 8, :]
                for r in range(1, 4):
                    value = jnp.where(group == r, modes_ref[row + 8 * r : row + 8 * r + 8, :], value)
                row = (b * 2 + s) * 8
                rows_ref[row : row + 8, q * 128 : (q + 1) * 128] = value
    first = which_ref[0] * 8
    for p in range(8):
        real = weight_ref[first + p, 0].astype(F32)
        imag = weight_ref[first + p, 1].astype(F32)
        for b in range(2):
            d0 = rows_ref[b * 16 + p : b * 16 + p + 1, :]
            d1 = rows_ref[b * 16 + 8 + p : b * 16 + 8 + p + 1, :]
            total0 = real * d0 + imag * d1
            total1 = real * d1 - imag * d0
            for s, total in enumerate((total0, total1)):
                folded = sum(total[:, q * 128 : (q + 1) * 128] for q in range(4))
                folded = folded + pltpu.roll(folded, 64, 1)
                folded = folded + pltpu.roll(folded, 32, 1)
                for half in range(2):
                    mixed_ref[pl.ds((half * 2 + b) * 128 + s * 64 + p, 8, stride=8), :] = (
                        folded[half * 8 : half * 8 + 8] * SCALE_F
                    )

    def mixed(half, b):
        row = (half * 2 + b) * 128
        return mixed_ref[row : row + 128, :]

    x_inverse(mixed, txi_ref, out_ref)


def spec_kernel(which_ref, u_ref, v_ref, d_ref, e_ref, out_ref):
    mine = which_ref[0] * 8
    other = 8 - mine
    for start, modes_ref, rows_ref in ((mine, u_ref, d_ref), (other, v_ref, e_ref)):
        for p in range(8):
            for half in range(2):
                u = [
                    [
                        modes_ref[pl.ds((half * 2 + b) * 128 + s * 64 + p, 8, stride=8), :] * SCALE_W
                        for s in range(2)
                    ]
                    for b in range(2)
                ]
                for q in range(4):
                    real = imag = 0.0
                    for b in range(2):
                        d0 = rows_ref[b * 16 + p : b * 16 + p + 1, q * 128 : (q + 1) * 128]
                        d1 = rows_ref[b * 16 + 8 + p : b * 16 + 9 + p, q * 128 : (q + 1) * 128]
                        real = real + (u[b][0] * d0 + u[b][1] * d1)
                        imag = imag + (u[b][0] * d1 - u[b][1] * d0)
                    lanes = slice(q * 128, (q + 1) * 128)
                    out_ref[start + p, 0, half * 8 : half * 8 + 8, lanes] = real
                    out_ref[start + p, 1, half * 8 : half * 8 + 8, lanes] = imag


def point_kernel(field_ref, dpre_ref, bias_ref, out_ref, acc_ref):
    x = pl.program_id(0)

    @pl.when(x == 0)
    def _():
        acc_ref[...] = jnp.zeros_like(acc_ref)

    acc_ref[...] += dot_nt(y_blocks(field_ref), y_blocks(dpre_ref))

    @pl.when(x == X - 1)
    def _():
        row = lax.broadcasted_iota(jnp.int32, (256, 256), 0) % 16
        column = lax.broadcasted_iota(jnp.int32, (256, 256), 1) % 16
        kept = jnp.where(row == column, acc_ref[...], 0.0)
        left = lax.broadcasted_iota(jnp.int32, (256, 128), 0) // 16
        fold = jnp.where(left == lax.broadcasted_iota(jnp.int32, (256, 128), 1), 1.0, 0.0)
        rows = jnp.concatenate(
            [jnp.sum(kept[i * 16 : (i + 1) * 16], axis=0, keepdims=True) for i in range(16)], axis=0
        )
        out_ref[0:16, :] = jnp.dot(
            rows, fold, preferred_element_type=F32, precision=lax.Precision.HIGHEST
        )
        lane = lax.broadcasted_iota(jnp.int32, (8, 128), 1)
        even = jnp.sum(bias_ref[:, 0:128], axis=1, keepdims=True)
        odd = jnp.sum(bias_ref[:, 128:256], axis=1, keepdims=True)
        out_ref[16:24, :] = jnp.where(lane == 0, even, jnp.where(lane == 1, odd, 0.0))


def whole(shape):
    return pl.BlockSpec(shape, lambda *_: (0,) * len(shape))


def by_plane():
    return pl.BlockSpec((None, C, NY, NZ), lambda x: (x, 0, 0, 0))


def by_plane_given():
    return pl.BlockSpec((None, C, None, NY, NZ), lambda x: (0, 0, x, 0, 0))


SMEM = pl.BlockSpec(memory_space=pltpu.SMEM)
BUFFER = (128, 16, 128)
GROUPED = (SLABS, 2, 16, 128)
PLANES = (X, C, NY, NZ)


def call(kernel, out_shape, grid, in_specs, out_specs, scratch, flops, moved, limit, name):
    return pl.pallas_call(
        kernel,
        out_shape=out_shape,
        grid=grid,
        in_specs=in_specs,
        out_specs=out_specs,
        scratch_shapes=scratch,
        compiler_params=pltpu.CompilerParams(vmem_limit_bytes=limit * MIB),
        cost_estimate=pl.CostEstimate(flops=flops, bytes_accessed=moved, transcendentals=0),
        name=name,
    )


def struct(shape, dtype):
    return jax.ShapeDtypeStruct(shape, dtype)


def exchange(buffer):
    return lax.all_to_all(buffer, BOTH, 0, 0, tiled=True)


def slab_index(x, z, y, c):
    return ((x * 2 + z) * 4 + y) * 2 + c


def total_over_devices(value):
    sizes = (4, 2, 4, 2)
    places = [(x, z, y, c) for x in range(4) for z in range(2) for y in range(4) for c in range(2)]
    for axis, step in ((3, 1), (2, 1), (2, 2), (0, 1), (0, 2), (1, 1)):
        pairs = []
        for place in places:
            other = list(place)
            other[axis] = (other[axis] ^ step) % sizes[axis]
            pairs.append((slab_index(*place), slab_index(*other)))
        value = value + lax.ppermute(value, "slab", pairs)
    return value + lax.ppermute(value, "batch", [(0, 1), (1, 0)])


def body(field, cotangent, spectral_weight, point_weight, point_bias):
    ty, tyt, zb, tx, txi = (jnp.asarray(t) for t in tables())
    which = lax.axis_index("batch").astype(jnp.int32).reshape(1)
    eye = jnp.eye(16, dtype=BF16)
    kron = jnp.kron(point_weight.T, eye)
    kron_back = jnp.kron(point_weight, eye)
    bias_column = jnp.repeat(point_bias, 16).reshape(256, 1)
    zf = pltpu.VMEM((2048, 512), BF16)
    planes = pltpu.VMEM((512, 2048), BF16)
    wide = pltpu.VMEM((2048, 128), F32)
    gather = pltpu.VMEM((512, 512), BF16)
    table_specs = {"ty": whole((64, NY)), "tyt": whole((NY, 64)), "zb": whole((256, 512))}
    big = 8 * MIB

    sent = call(
        field_kernel, struct(BUFFER, BF16), (X,),
        [by_plane_given(), table_specs["ty"], table_specs["zb"]], whole(BUFFER),
        [zf, planes, wide], 2 * 10**9, big, 32, "field_planes",
    )(field, ty, zb)
    got = exchange(sent)
    pre = call(
        pre_kernel, struct(PLANES, BF16), (X,),
        [by_plane_given(), whole((256, 256)), whole((256, 1))], by_plane(),
        [], 2 * 10**9, 2 * big, 32, "point_map",
    )(field, kron, bias_column)
    back, modes_u = call(
        mix_kernel, (struct(GROUPED, BF16), struct((512, 128), F32)), (),
        [SMEM] + [pl.BlockSpec(memory_space=pltpu.VMEM)] * 4,
        (pl.BlockSpec(memory_space=pltpu.VMEM),) * 2,
        [pltpu.VMEM((32, 512), F32)], 10**9, 3 * MIB, 32, "mix_modes",
    )(which, got.reshape(GROUPED), spectral_weight, tx, txi)
    got = exchange(back.reshape(BUFFER))
    other_u = lax.ppermute(modes_u, "batch", [(0, 1), (1, 0)])
    dpre, sent, bias_rows = call(
        signal_kernel,
        (struct(PLANES, BF16), struct(BUFFER, BF16), struct((8, 256), F32)), (X,),
        [whole(BUFFER), by_plane(), by_plane_given(), table_specs["ty"], table_specs["tyt"],
         table_specs["zb"]],
        (by_plane(), whole(BUFFER), whole((8, 256))),
        [zf, planes, wide, gather, planes], 6 * 10**9, 3 * big, 48, "signal",
    )(got, pre, cotangent, ty, tyt, zb)
    got = exchange(sent)
    partial = call(
        point_kernel, struct((24, 128), F32), (X,),
        [by_plane_given(), by_plane(), whole((8, 256))], whole((24, 128)),
        [pltpu.VMEM((256, 256), F32)], 2 * 10**9, 2 * big, 32, "point_gradient",
    )(field, dpre, bias_rows)
    totals = total_over_devices(partial)
    back, rows_d = call(
        adjoint_kernel, (struct(GROUPED, BF16), struct((32, 512), F32)), (),
        [SMEM] + [pl.BlockSpec(memory_space=pltpu.VMEM)] * 4,
        (pl.BlockSpec(memory_space=pltpu.VMEM),) * 2,
        [pltpu.VMEM((512, 128), F32), pltpu.VMEM((512, 128), F32)],
        10**9, 3 * MIB, 32, "adjoint_modes",
    )(which, got.reshape(GROUPED), spectral_weight, tx, txi)
    got = exchange(back.reshape(BUFFER))
    other_d = lax.ppermute(rows_d, "batch", [(0, 1), (1, 0)])
    mapped = call(
        back_kernel, struct(PLANES, BF16), (X,),
        [by_plane(), whole((256, 256))], by_plane(),
        [], 2 * 10**9, 2 * big, 32, "point_map_back",
    )(dpre, kron_back)
    grad_spec = call(
        spec_kernel, struct((16, 2, C, 512), F32), (),
        [SMEM] + [pl.BlockSpec(memory_space=pltpu.VMEM)] * 4,
        pl.BlockSpec(memory_space=pltpu.VMEM),
        [], 10**7, 2 * MIB, 32, "spectral_gradient",
    )(which, modes_u, other_u, rows_d, other_d)
    input_grad = call(
        final_kernel, struct((1, C, X, NY, NZ), BF16), (X,),
        [whole(BUFFER), by_plane(), table_specs["tyt"], table_specs["zb"]], by_plane_given(),
        [zf, wide, gather, planes], 4 * 10**9, 2 * big, 48, "input_gradient",
    )(got, mapped, tyt, zb)
    grad_point = (0.5 * SCALE_P) * totals[:16, :16]
    grad_bias = (0.5 * SCALE_P) * totals[16:24, :2].reshape(16)
    return input_grad, grad_spec, grad_point, grad_bias


def solution(mesh):
    planes = P("batch", None, "slab", None, None)
    return jax.shard_map(
        body,
        mesh=mesh,
        in_specs=(planes, planes, P("slab", None, None, None), P(), P()),
        out_specs=(planes, P("slab", None, None, None), P(), P()),
        check_vma=False,
    )
```

```python
import math

import jax
import jax.numpy as jnp
import numpy as np
from jax import lax
from jax.experimental import pallas as pl
from jax.experimental.pallas import tpu as pltpu
from jax.sharding import PartitionSpec as P

C = 16
X = 8
NY = 256
NZ = 128
NX = 512
MODES = 32
SLABS = 64
CELLS = NX * NY * NZ
SCALE_F = 1.0 / math.sqrt(CELLS)
SCALE_I = 1.0 / math.sqrt(MODES**3)
SCALE_P = 1.0 / math.sqrt(2 * CELLS)
SCALE_W = math.sqrt(MODES**3 / (2 * CELLS))
GELU_A = math.sqrt(2.0 / math.pi)
GK = (GELU_A * 0.044715) ** (1.0 / 3.0)
GA = GELU_A / GK
BOTH = ("slab", "batch")
F32 = jnp.float32
BF16 = jnp.bfloat16
MIB = 1 << 20
LIMIT = 48
CUT = 2


def freqs(number, length):
    index = np.arange(number)
    return np.where(index < number // 2, index, index + length - number)


def angles(length, frequencies):
    product = (np.arange(length)[:, None] * frequencies[None, :]) % length
    return product * (2.0 * math.pi / length)


def tables():
    thy = angles(NY, freqs(MODES, NY))
    thz = angles(NZ, np.arange(MODES))
    thx = angles(NX, freqs(MODES, NX))
    ty = np.concatenate([np.cos(thy).T, -np.sin(thy).T], axis=0)
    cos, sin = np.cos(thz), np.sin(thz)
    rot = np.zeros((2, NZ, 2, MODES))
    rot[0, :, 0], rot[1, :, 0] = cos, sin
    rot[1, :, 1], rot[0, :, 1] = cos, -sin
    zb = rot.reshape(2, NZ, 2, 2, 2, 8).transpose(0, 1, 3, 2, 4, 5)
    zb = np.stack([zb, zb[:, :, :, :, ::-1]], axis=2)[:, :, :, :, :, :, None, :]
    zb = np.broadcast_to(zb, (2, NZ, 2, 2, 2, 2, 4, 8)).reshape(2 * NZ, 512)
    cs = np.stack([np.cos(thx), np.sin(thx)]).reshape(2, SLABS, X, MODES)
    tx = np.zeros((2, 2, 4, MODES, SLABS, 2, X))
    txi = np.zeros((SLABS, 2, X, 2, 2, MODES))
    for half in range(2):
        tx[half, :, :, :, :, half] = cs.transpose(0, 3, 1, 2)[:, None]
        txi[:, half, :, half] = cs.transpose(1, 2, 0, 3)
    return tuple(
        np.asarray(t, np.float32).astype(BF16)
        for t in (ty, ty.T, zb, tx.reshape(512, 1024), txi.reshape(1024, 128))
    )


def dot(left, right):
    return jnp.dot(left, right, preferred_element_type=F32)


def dot_nt(left, right):
    return lax.dot_general(left, right, (((1,), (1,)), ((), ())), preferred_element_type=F32)


def build_z(zb_ref, zf_ref):
    channel = (lax.broadcasted_iota(jnp.int32, (2 * NZ, 256), 1) // 8) % 4
    for group in range(2):
        table = zb_ref[:, group * 256 : (group + 1) * 256].astype(F32)
        for c in range(4):
            row = group * 1024 + c * 256
            zf_ref[row : row + 256, :] = jnp.where(channel == c, table, 0.0).astype(BF16)


def low_lanes(rows):
    return lax.broadcasted_iota(jnp.int32, (rows, 128), 1) % 64 < 32


def z_forward(planes_ref, zf_ref, wide_ref, out_ref):
    low = low_lanes(256)
    for half in range(2):
        first, second = (
            dot(
                planes_ref[half * 256 : (half + 1) * 256, group * 1024 : (group + 1) * 1024],
                zf_ref[group * 1024 : (group + 1) * 1024, :],
            )
            for group in range(2)
        )
        for t in range(2):
            one, two = first[:, t * 128 : (t + 1) * 128], second[:, t * 128 : (t + 1) * 128]
            for j, value in enumerate((jnp.where(low, one, two), jnp.where(low, two, one))):
                for x in range(X):
                    wide_ref[pl.ds((2 * t + j) * 16 + half * 8 + x, 32, stride=64), :] = value[
                        x * 32 : (x + 1) * 32
                    ]
    out_ref[...] = wide_ref[...].astype(BF16).reshape(128, 16, 128)


def z_inverse(in_ref, zf_ref, wide_ref, gather_ref, rolled_ref):
    rows = in_ref.shape[1]
    wide_ref[...] = in_ref[...].astype(F32).reshape(128 * rows, 128)
    low = low_lanes(32)
    for half in range(2):
        for x in range(X):
            row = (half * 8 + x) * 32
            for t in range(2):
                even, odd = (
                    wide_ref[pl.ds((2 * t + j) * rows + half * 8 + x, 32, stride=4 * rows), :]
                    for j in range(2)
                )
                for group, value in enumerate((jnp.where(low, even, odd), jnp.where(low, odd, even))):
                    column = group * 256 + t * 128
                    gather_ref[row : row + 32, column : column + 128] = value.astype(BF16)
    for c in range(8):
        group = c // 4
        rolled_ref[:, c * 256 : (c + 1) * 256] = dot_nt(
            gather_ref[:, group * 256 : (group + 1) * 256], zf_ref[c * 256 : (c + 1) * 256, :]
        ).astype(BF16)


def y_forward(ty_ref, pair, planes_ref, x, op):
    result = dot(ty_ref[...], pair)
    half, first = op // 4, (op % 4) * 2
    rows = pl.ds(pl.multiple_of(half * 256 + x * 32, 32), 32)
    for j in range(2):
        for part in range(2):
            column = (first + j) * 256 + part * 128
            planes_ref[rows, column : column + 128] = result[
                part * 32 : (part + 1) * 32, j * 128 : (j + 1) * 128
            ].astype(BF16)
    return result


def y_inverse(tyt_ref, rolled_ref, x, op):
    half, first = op // 4, (op % 4) * 2
    rows = pl.ds(pl.multiple_of(half * 256 + x * 32, 32), 32)
    blocks = []
    for j in range(2):
        column = (first + j) * 256
        blocks.append(
            jnp.concatenate(
                [
                    rolled_ref[rows, column : column + 128],
                    rolled_ref[rows, column + 128 : column + 256],
                ],
                axis=0,
            )
        )
    return dot(tyt_ref[...], jnp.concatenate(blocks, axis=1))


class Planes:
    def __init__(self, hbm_ref, vmem_ref, sem, given, out=False):
        self.hbm_ref, self.vmem_ref, self.sem, self.given, self.out = hbm_ref, vmem_ref, sem, given, out

    def copy(self, x, channels):
        far = self.hbm_ref.at[0, channels, x] if self.given else self.hbm_ref.at[x, channels]
        near = self.vmem_ref.at[x, channels]
        source, target = (near, far) if self.out else (far, near)
        return pltpu.make_async_copy(source, target, self.sem.at[x])

    def start(self, x):
        for c in range(0, C, CUT):
            self.copy(x, pl.ds(c, CUT)).start()

    def wait(self, x):
        self.copy(x, pl.ds(0, C)).wait()


def field_kernel(
    field_hbm, ty_hbm, zb_hbm, out_ref,
    zf_ref, planes_ref, wide_ref, field_ref, ty_ref, zb_ref, sem, ty_sem, zb_sem,
):
    load = Planes(field_hbm, field_ref, sem, True)
    load_ty = pltpu.make_async_copy(ty_hbm, ty_ref, ty_sem)
    load_zb = pltpu.make_async_copy(zb_hbm, zb_ref, zb_sem)
    load_ty.start()
    load.start(0)
    load_zb.start()
    for x in range(1, X):
        load.start(x)
    load_ty.wait()
    load_zb.wait()
    build_z(zb_ref, zf_ref)

    def step(x, _):
        load.wait(x)
        for op in range(8):
            pair = jnp.concatenate([field_ref[x, 2 * op], field_ref[x, 2 * op + 1]], axis=1)
            y_forward(ty_ref, pair, planes_ref, x, op)
        return 0

    lax.fori_loop(0, X, step, 0)
    z_forward(planes_ref, zf_ref, wide_ref, out_ref)


def y_blocks(ref, x):
    return jnp.concatenate(
        [ref[x, :, b * 16 : (b + 1) * 16, :].reshape(256, 128) for b in range(16)], axis=1
    )


def owner_rows():
    group = lax.broadcasted_iota(jnp.int32, (256, 16), 0) // 16
    return jnp.where(group == lax.broadcasted_iota(jnp.int32, (256, 16), 1), 1.0, 0.0)


def same_row(value):
    row = lax.broadcasted_iota(jnp.int32, (256, 256), 0) % 16
    column = lax.broadcasted_iota(jnp.int32, (256, 256), 1) % 16
    return jnp.where(row == column, value, 0.0)


def map_planes(scale, in_hbm, map_rows, bias, out_hbm, in_ref, out_ref, in_sem, out_sem):
    load = Planes(in_hbm, in_ref, in_sem, len(in_hbm.shape) == 5)
    store = Planes(out_hbm, out_ref, out_sem, False, True)
    for x in range(X):
        load.start(x)
    kron = same_row(dot_nt(map_rows.astype(BF16), owner_rows().astype(BF16))).astype(BF16)

    def step(x, _):
        load.wait(x)
        for b in range(8):
            pair = jnp.concatenate(
                [in_ref[x, :, y : y + 16, :].reshape(256, 128) for y in (b * 32, b * 32 + 16)],
                axis=1,
            )
            result = dot(kron, pair)
            if bias is not None:
                result = result + bias
            result = (result * scale).astype(BF16)
            for j in range(2):
                y = b * 32 + j * 16
                out_ref[x, :, y : y + 16, :] = result[:, j * 128 : (j + 1) * 128].reshape(C, 16, 128)
        store.start(x)
        return 0

    lax.fori_loop(0, X, step, 0)
    for x in range(X):
        store.wait(x)


def pre_kernel(in_hbm, weight_ref, bias_ref, out_hbm, in_ref, out_ref, in_sem, out_sem):
    map_rows = dot_nt(owner_rows().astype(BF16), weight_ref[...])
    bias = jnp.sum(owner_rows() * bias_ref[...], axis=1, keepdims=True)
    map_planes(GK, in_hbm, map_rows, bias, out_hbm, in_ref, out_ref, in_sem, out_sem)


def back_kernel(in_hbm, weight_ref, out_hbm, in_ref, out_ref, in_sem, out_sem):
    map_rows = dot(owner_rows().astype(BF16), weight_ref[...])
    map_planes(0.5, in_hbm, map_rows, None, out_hbm, in_ref, out_ref, in_sem, out_sem)


def slope_of(h):
    one, add = BF16(1.0), BF16(GA)
    square = h * h
    t = jnp.tanh(h * (square + add))
    slope = h * (square * BF16(3.0) + add)
    return (one + t) * (one + (one - t) * slope)


def signal_kernel(
    in_ref, pre_hbm, cot_hbm, ty_ref, tyt_ref, zb_ref,
    dpre_hbm, out_ref, bias_ref,
    zf_ref, planes_ref, wide_ref, gather_ref, rolled_ref, pre_ref, cot_ref,
    pre_sem, cot_sem, out_sem,
):
    load_pre = Planes(pre_hbm, pre_ref, pre_sem, False)
    load_cot = Planes(cot_hbm, cot_ref, cot_sem, True)
    store = Planes(dpre_hbm, cot_ref, out_sem, False, True)
    for x in range(X):
        load_pre.start(x)
        load_cot.start(x)
    build_z(zb_ref, zf_ref)
    z_inverse(in_ref, zf_ref, wide_ref, gather_ref, rolled_ref)
    bias_ref[...] = jnp.zeros_like(bias_ref)

    def step(x, _):
        load_pre.wait(x)
        load_cot.wait(x)
        for op in range(8):
            back = y_inverse(tyt_ref, rolled_ref, x, op)
            for j in range(2):
                o = 2 * op + j
                h = back[:, j * 128 : (j + 1) * 128].astype(BF16) + pre_ref[x, o]
                cot_ref[x, o] = slope_of(h) * cot_ref[x, o]
        store.start(x)
        for op in range(8):
            pair = jnp.concatenate([cot_ref[x, 2 * op], cot_ref[x, 2 * op + 1]], axis=1)
            result = y_forward(ty_ref, pair, planes_ref, x, op)
            bias_ref[op : op + 1, :] += result[0:1, :]
        return 0

    lax.fori_loop(0, X, step, 0)
    z_forward(planes_ref, zf_ref, wide_ref, out_ref)
    for x in range(X):
        store.wait(x)


def final_kernel(
    in_ref, mapped_hbm, tyt_ref, zb_ref, out_hbm, point_ref, bias_ref,
    zf_ref, wide_ref, gather_ref, rolled_ref, mapped_ref, out_ref, in_sem, out_sem,
):
    load = Planes(mapped_hbm, mapped_ref, in_sem, False)
    store = Planes(out_hbm, out_ref, out_sem, True, True)
    for x in range(X):
        load.start(x)
    build_z(zb_ref, zf_ref)
    z_inverse(in_ref, zf_ref, wide_ref, gather_ref, rolled_ref)

    def step(x, _):
        load.wait(x)
        for op in range(8):
            back = y_inverse(tyt_ref, rolled_ref, x, op)
            for j in range(2):
                o = 2 * op + j
                mapped = mapped_ref[x, o].astype(F32)
                out_ref[x, o] = (back[:, j * 128 : (j + 1) * 128] + mapped).astype(BF16)
        store.start(x)
        return 0

    lax.fori_loop(0, X, step, 0)
    total = jnp.sum(wide_ref[...].reshape(128, 24, 128)[:, 16:24, :], axis=0) * (0.5 * SCALE_P)
    lane = lax.broadcasted_iota(jnp.int32, (16, 128), 1)
    row = lax.broadcasted_iota(jnp.int32, (16, 128), 0)
    point = jnp.where(row < 8, total[0:1] + total[2:3], total[1:2] + total[3:4])
    point = jnp.where(lane // 16 == row % 8, point, 0.0)
    bias = jnp.where(lane < 32, total[4:5], 0.0)
    fold = lax.broadcasted_iota(jnp.int32, (128, 16), 0) % 16
    fold = jnp.where(fold == lax.broadcasted_iota(jnp.int32, (128, 16), 1), 1.0, 0.0)
    exact = lax.Precision.HIGHEST
    point_ref[...] = jnp.dot(point, fold, preferred_element_type=F32, precision=exact)
    bias_ref[...] = jnp.dot(bias, fold, preferred_element_type=F32, precision=exact)[0:1]
    for x in range(X):
        store.wait(x)


def swapped(which, w):
    return which + w * (1 - 2 * which)


def x_forward(which, in_ref, tx_ref, scale, modes_ref):
    data = jnp.concatenate([in_ref[:, b].reshape(1024, 128) for b in range(2)], axis=1)
    raw = dot(tx_ref[...], data)
    lane = lax.broadcasted_iota(jnp.int32, (128, 128), 1)
    sign = jnp.where(lane < 64, scale, -scale)
    for half in range(2):
        for b in range(2):
            cosine = raw[half * 256 : half * 256 + 128, b * 128 : (b + 1) * 128]
            sine = raw[half * 256 + 128 : half * 256 + 256, b * 128 : (b + 1) * 128]
            modes = cosine * scale + pltpu.roll(sine, 64, 1) * sign
            turned = modes.T
            for s in range(2):
                for w in range(2):
                    row = (half * 2 + b) * 128 + s * 64 + swapped(which, w) * 32
                    place = s * 64 + w * 32
                    modes_ref[pl.ds(pl.multiple_of(row, 32), 32), :] = turned[place : place + 32]


def x_inverse(mixed, txi_ref, out_ref, extra):
    lane = lax.broadcasted_iota(jnp.int32, (32, 128), 1)
    rows = []
    for half in range(2):
        turned = [mixed(half, b).T[:32] for b in range(2)]
        rows.append(jnp.concatenate(turned, axis=1))
        rows.append(
            jnp.concatenate(
                [jnp.where(lane < 64, -1.0, 1.0) * pltpu.roll(g, 64, 1) for g in turned], axis=1
            )
        )
    result = dot(txi_ref[...], jnp.concatenate(rows, axis=0).astype(BF16))
    for b in range(2):
        block = result[:, b * 128 : (b + 1) * 128].reshape(SLABS, 16, 128)
        if extra is not None:
            block = jnp.concatenate(
                [block, jnp.broadcast_to(extra[None], (SLABS, 8, 128))], axis=1
            )
        out_ref[:, b] = block.astype(BF16)


def mix_kernel(which_ref, in_ref, weight_ref, tx_ref, txi_ref, out_ref, modes_ref, mixed_ref):
    which = which_ref[0]
    x_forward(which, in_ref, tx_ref, SCALE_F, modes_ref)
    first = which * 8
    for p in range(8):
        real = weight_ref[first + p, 0].astype(F32)
        imag = weight_ref[first + p, 1].astype(F32)
        for b in range(2):
            u = [
                [modes_ref[pl.ds((half * 2 + b) * 128 + s * 64 + p, 8, stride=8), :] for s in range(2)]
                for half in range(2)
            ]
            for q in range(4):
                total = [0.0, 0.0]
                for half in range(2):
                    w0 = real[half * 8 : half * 8 + 8, q * 128 : (q + 1) * 128]
                    w1 = imag[half * 8 : half * 8 + 8, q * 128 : (q + 1) * 128]
                    u0, u1 = u[half]
                    total[0] = total[0] + (u0 * w0 - u1 * w1)
                    total[1] = total[1] + (u0 * w1 + u1 * w0)
                for s in range(2):
                    row = (b * 2 + s) * 8 + p
                    mixed_ref[row : row + 1, q * 128 : (q + 1) * 128] = jnp.sum(
                        total[s], axis=0, keepdims=True
                    ) * (SCALE_I * GK)

    def mixed(half, b):
        pieces = []
        for s in range(2):
            row = (b * 2 + s) * 8
            for w in range(2):
                column = pl.multiple_of((half * 2 + swapped(which, w)) * 128, 128)
                piece = mixed_ref[row : row + 8, pl.ds(column, 128)]
                for r in range(4):
                    pieces.append(pltpu.roll(piece, 128 - 32 * r, 1) if r else piece)
        return jnp.concatenate(pieces, axis=0)

    x_inverse(mixed, txi_ref, out_ref, None)


def adjoint_kernel(
    which_ref, in_ref, weight_ref, tx_ref, txi_ref, extra_ref,
    out_ref, rows_ref, modes_ref, mixed_ref,
):
    which = which_ref[0]
    x_forward(which, in_ref, tx_ref, 0.5 * SCALE_I, modes_ref)
    group = lax.broadcasted_iota(jnp.int32, (8, 128), 1) // 32
    for b in range(2):
        for s in range(2):
            for q in range(4):
                half, c = q // 2, (q % 2) * 4
                row = (half * 2 + b) * 128 + s * 64 + c * 8
                value = modes_ref[row : row + 8, :]
                for r in range(1, 4):
                    value = jnp.where(group == r, modes_ref[row + 8 * r : row + 8 * r + 8, :], value)
                row = (b * 2 + s) * 8
                rows_ref[row : row + 8, q * 128 : (q + 1) * 128] = value
    first = which * 8
    for p in range(8):
        real = weight_ref[first + p, 0].astype(F32)
        imag = weight_ref[first + p, 1].astype(F32)
        for b in range(2):
            d0 = rows_ref[b * 16 + p : b * 16 + p + 1, :]
            d1 = rows_ref[b * 16 + 8 + p : b * 16 + 8 + p + 1, :]
            total0 = real * d0 + imag * d1
            total1 = real * d1 - imag * d0
            for s, total in enumerate((total0, total1)):
                folded = sum(total[:, q * 128 : (q + 1) * 128] for q in range(4))
                folded = folded + pltpu.roll(folded, 64, 1)
                folded = folded + pltpu.roll(folded, 32, 1)
                for half in range(2):
                    mixed_ref[pl.ds((half * 2 + b) * 128 + s * 64 + p, 8, stride=8), :] = (
                        folded[half * 8 : half * 8 + 8] * SCALE_F
                    )

    def mixed(half, b):
        pieces = []
        for s in range(2):
            for w in range(2):
                row = (half * 2 + b) * 128 + s * 64 + swapped(which, w) * 32
                pieces.append(mixed_ref[pl.ds(pl.multiple_of(row, 32), 32), :])
        return jnp.concatenate(pieces, axis=0)

    x_inverse(mixed, txi_ref, out_ref, extra_ref[...])


def spec_kernel(which_ref, u_ref, v_bf_ref, d_ref, e_bf_ref, out_ref, v_ref, e_ref):
    v_ref[...] = v_bf_ref[...].astype(F32)
    e_ref[...] = e_bf_ref[...].astype(F32)
    mine = which_ref[0] * 8
    other = 8 - mine
    for start, modes_ref, rows_ref in ((mine, u_ref, d_ref), (other, v_ref, e_ref)):
        for p in range(8):
            for half in range(2):
                u = [
                    [
                        modes_ref[pl.ds((half * 2 + b) * 128 + s * 64 + p, 8, stride=8), :] * SCALE_W
                        for s in range(2)
                    ]
                    for b in range(2)
                ]
                for q in range(4):
                    real = imag = 0.0
                    for b in range(2):
                        d0 = rows_ref[b * 16 + p : b * 16 + p + 1, q * 128 : (q + 1) * 128]
                        d1 = rows_ref[b * 16 + 8 + p : b * 16 + 9 + p, q * 128 : (q + 1) * 128]
                        real = real + (u[b][0] * d0 + u[b][1] * d1)
                        imag = imag + (u[b][0] * d1 - u[b][1] * d0)
                    lanes = slice(q * 128, (q + 1) * 128)
                    out_ref[start + p, 0, half * 8 : half * 8 + 8, lanes] = real
                    out_ref[start + p, 1, half * 8 : half * 8 + 8, lanes] = imag


def point_kernel(
    field_hbm, dpre_hbm, bias_ref, out_ref, acc_ref, field_ref, dpre_ref, field_sem, dpre_sem
):
    load_field = Planes(field_hbm, field_ref, field_sem, True)
    load_dpre = Planes(dpre_hbm, dpre_ref, dpre_sem, False)
    for x in range(X):
        load_field.start(x)
        load_dpre.start(x)
    acc_ref[...] = jnp.zeros_like(acc_ref)

    def step(x, _):
        load_field.wait(x)
        load_dpre.wait(x)
        acc_ref[...] += dot_nt(y_blocks(field_ref, x), y_blocks(dpre_ref, x))
        return 0

    lax.fori_loop(0, X, step, 0)
    kept = same_row(acc_ref[...])
    rows = jnp.concatenate(
        [jnp.sum(kept[i * 16 : (i + 1) * 16], axis=0, keepdims=True) for i in range(16)], axis=0
    )
    owner = lax.broadcasted_iota(jnp.int32, (256, 128), 0) // 16
    column = lax.broadcasted_iota(jnp.int32, (256, 128), 1) % 16
    point = jnp.dot(
        rows,
        jnp.where(owner == column, 1.0, 0.0),
        preferred_element_type=F32,
        precision=lax.Precision.HIGHEST,
    )
    lane = lax.broadcasted_iota(jnp.int32, (8, 128), 1)
    row = lax.broadcasted_iota(jnp.int32, (8, 128), 0)
    first, second = (
        jnp.sum(jnp.where(lane // 16 == row, point[h * 8 : h * 8 + 8], 0.0), axis=0, keepdims=True)
        for h in range(2)
    )
    even = jnp.sum(bias_ref[:, 0:128], axis=1, keepdims=True)
    odd = jnp.sum(bias_ref[:, 128:256], axis=1, keepdims=True)
    bias = jnp.where(lane == 2 * row, even, jnp.where(lane == 2 * row + 1, odd, 0.0))
    bias = jnp.sum(bias, axis=0, keepdims=True)
    value = jnp.where(
        (row == 0) | (row == 2), first, jnp.where((row == 1) | (row == 3), second, 0.0)
    )
    value = jnp.where(row == 4, bias, value)
    high = value.astype(BF16).astype(F32)
    low = value - high
    packed = jnp.where(row < 2, high, jnp.where(row < 4, low, 0.0))
    packed = jnp.where((row == 4) & (lane < 16), high, packed)
    out_ref[...] = jnp.where((row == 4) & (lane >= 16), pltpu.roll(low, 16, 1), packed)


SMEM = pl.BlockSpec(memory_space=pltpu.SMEM)
VMEM = pl.BlockSpec(memory_space=pltpu.VMEM)
HBM = pl.BlockSpec(memory_space=pltpu.HBM)
BUFFER = (128, 16, 128)
PLANES = (X, C, NY, NZ)
GIVEN = (1, C, X, NY, NZ)


def struct(shape, dtype):
    return jax.ShapeDtypeStruct(shape, dtype)


def call(kernel, out_shape, in_specs, out_specs, scratch, flops, moved, limit, name):
    return pl.pallas_call(
        kernel,
        out_shape=out_shape,
        in_specs=in_specs,
        out_specs=out_specs,
        scratch_shapes=scratch,
        compiler_params=pltpu.CompilerParams(vmem_limit_bytes=limit * MIB),
        cost_estimate=pl.CostEstimate(flops=flops, bytes_accessed=moved, transcendentals=0),
        name=name,
    )


def exchange(buffer):
    return lax.all_to_all(buffer, BOTH, 0, 0, tiled=True)


def grouped(buffer):
    return buffer.reshape((SLABS, 2) + buffer.shape[1:])


def flat(buffer):
    return buffer.reshape((128,) + buffer.shape[2:])


def body(field, cotangent, spectral_weight, point_weight, point_bias):
    ty, tyt, zb, tx, txi = (jnp.asarray(t) for t in tables())
    which = lax.axis_index("batch").astype(jnp.int32).reshape(1)
    zf = pltpu.VMEM((2048, 256), BF16)
    planes = pltpu.VMEM((512, 2048), BF16)
    wide = pltpu.VMEM((2048, 128), F32)
    gather = pltpu.VMEM((512, 512), BF16)
    held = pltpu.VMEM(PLANES, BF16)
    sems = pltpu.SemaphoreType.DMA((X,))
    big = 8 * MIB
    swap = [(0, 1), (1, 0)]

    sent = call(
        field_kernel, struct(BUFFER, BF16), [HBM, HBM, HBM], VMEM,
        [zf, planes, wide, held, pltpu.VMEM((64, NY), BF16), pltpu.VMEM((256, 512), BF16), sems,
         pltpu.SemaphoreType.DMA, pltpu.SemaphoreType.DMA], 2 * 10**9, big, 60, "field_planes",
    )(field, ty, zb)
    got = exchange(sent)
    pre = call(
        pre_kernel, struct(PLANES, BF16), [HBM, VMEM, VMEM], HBM,
        [held, held, sems, sems], 2 * 10**9, 2 * big, LIMIT, "point_map",
    )(field, point_weight, point_bias.reshape(1, C))
    got, pre = lax.optimization_barrier((got, pre))
    back, modes_u = call(
        mix_kernel, (struct((SLABS, 2, 16, 128), BF16), struct((512, 128), F32)),
        [SMEM] + [VMEM] * 4, (VMEM, VMEM),
        [pltpu.VMEM((32, 512), F32)], 10**9, 3 * MIB, 32, "mix_modes",
    )(which, grouped(got), spectral_weight, tx, txi)
    got = exchange(flat(back))
    other_u = lax.ppermute(modes_u.astype(BF16), "batch", swap)
    got, other_u = lax.optimization_barrier((got, other_u))
    dpre, sent, bias_rows = call(
        signal_kernel,
        (struct(PLANES, BF16), struct(BUFFER, BF16), struct((8, 256), F32)),
        [VMEM, HBM, HBM, VMEM, VMEM, VMEM], (HBM, VMEM, VMEM),
        [zf, planes, wide, gather, planes, held, held, sems, sems, sems],
        6 * 10**9, 3 * big, LIMIT, "signal",
    )(got, pre, cotangent, ty, tyt, zb)
    got = exchange(sent)
    extra = call(
        point_kernel, struct((8, 128), F32), [HBM, HBM, VMEM], VMEM,
        [pltpu.VMEM((256, 256), F32), held, held, sems, sems],
        2 * 10**9, 2 * big, LIMIT, "point_gradient",
    )(field, dpre, bias_rows)
    back, rows_d = call(
        adjoint_kernel, (struct((SLABS, 2, 24, 128), BF16), struct((32, 512), F32)),
        [SMEM] + [VMEM] * 5, (VMEM, VMEM),
        [pltpu.VMEM((512, 128), F32), pltpu.VMEM((512, 128), F32)],
        10**9, 3 * MIB, 32, "adjoint_modes",
    )(which, grouped(got), spectral_weight, tx, txi, extra)
    dpre, rows_d = lax.optimization_barrier((dpre, rows_d))
    got = exchange(flat(back))
    other_d = lax.ppermute(rows_d.astype(BF16), "batch", swap)
    mapped = call(
        back_kernel, struct(PLANES, BF16), [HBM, VMEM], HBM,
        [held, held, sems, sems], 2 * 10**9, 2 * big, LIMIT, "point_map_back",
    )(dpre, point_weight)
    grad_spec = call(
        spec_kernel, struct((16, 2, C, 512), F32), [SMEM] + [VMEM] * 4, VMEM,
        [pltpu.VMEM((512, 128), F32), pltpu.VMEM((32, 512), F32)],
        10**7, 2 * MIB, 32, "spectral_gradient",
    )(which, modes_u, other_u, rows_d, other_d)
    input_grad, grad_point, grad_bias = call(
        final_kernel, (struct(GIVEN, BF16), struct((C, C), F32), struct((1, C), F32)),
        [VMEM, HBM, VMEM, VMEM], (HBM, VMEM, VMEM),
        [zf, pltpu.VMEM((3072, 128), F32), gather, planes, held, held, sems, sems],
        4 * 10**9, 2 * big, LIMIT, "input_gradient",
    )(got, mapped, tyt, zb)
    return input_grad, grad_spec, grad_point, grad_bias.reshape(C)


def solution(mesh):
    planes = P("batch", None, "slab", None, None)
    return jax.shard_map(
        body,
        mesh=mesh,
        in_specs=(planes, planes, P("slab", None, None, None), P(), P()),
        out_specs=(planes, P("slab", None, None, None), P(), P()),
        check_vma=False,
    )
```

```python
import math

import jax
import jax.numpy as jnp
import numpy as np
from jax import lax
from jax.experimental import pallas as pl
from jax.experimental.pallas import tpu as pltpu
from jax.sharding import PartitionSpec as P

C = 16
X = 8
NY = 256
NZ = 128
NX = 512
MODES = 32
SLABS = 64
CELLS = NX * NY * NZ
SCALE_F = 1.0 / math.sqrt(CELLS)
SCALE_I = 1.0 / math.sqrt(MODES**3)
SCALE_P = 1.0 / math.sqrt(2 * CELLS)
SCALE_W = math.sqrt(MODES**3 / (2 * CELLS))
GELU_A = math.sqrt(2.0 / math.pi)
GK = (GELU_A * 0.044715) ** (1.0 / 3.0)
GA = GELU_A / GK
BOTH = ("slab", "batch")
F32 = jnp.float32
BF16 = jnp.bfloat16
MIB = 1 << 20
LIMIT = 48
CUT = 4
AHEAD = 4
PARTS = 8


def freqs(number, length):
    index = np.arange(number)
    return np.where(index < number // 2, index, index + length - number)


def angles(length, frequencies):
    product = (np.arange(length)[:, None] * frequencies[None, :]) % length
    return product * (2.0 * math.pi / length)


def tables():
    thy = angles(NY, freqs(MODES, NY))
    thz = angles(NZ, np.arange(MODES))
    thx = angles(NX, freqs(MODES, NX))
    ty = np.concatenate([np.cos(thy).T, -np.sin(thy).T], axis=0)
    cos, sin = np.cos(thz), np.sin(thz)
    rot = np.zeros((2, NZ, 2, MODES))
    rot[0, :, 0], rot[1, :, 0] = cos, sin
    rot[1, :, 1], rot[0, :, 1] = cos, -sin
    zb = rot.reshape(2, NZ, 2, 2, 2, 8).transpose(0, 1, 3, 2, 4, 5)
    zb = np.stack([zb, zb[:, :, :, :, ::-1]], axis=2)[:, :, :, :, :, :, None, :]
    zb = np.broadcast_to(zb, (2, NZ, 2, 2, 2, 2, 4, 8)).reshape(2 * NZ, 512)
    cs = np.stack([np.cos(thx), np.sin(thx)]).reshape(2, SLABS, X, MODES)
    tx = np.zeros((2, 2, 4, MODES, SLABS, 2, X))
    txi = np.zeros((SLABS, 2, X, 2, 2, MODES))
    for half in range(2):
        tx[half, :, :, :, :, half] = cs.transpose(0, 3, 1, 2)[:, None]
        txi[:, half, :, half] = cs.transpose(1, 2, 0, 3)
    return tuple(
        np.asarray(t, np.float32).astype(BF16)
        for t in (ty, ty.T, zb, tx.reshape(512, 1024), txi.reshape(1024, 128))
    )


def dot(left, right):
    return jnp.dot(left, right, preferred_element_type=F32)


def dot_nt(left, right):
    return lax.dot_general(left, right, (((1,), (1,)), ((), ())), preferred_element_type=F32)


def send_part(stage_ref, out_hbm, sem, i):
    count = out_hbm.shape[0] // PARTS
    part = pl.ds(i * count, count)
    return pltpu.make_async_copy(stage_ref.at[part], out_hbm.at[part], sem.at[i])


def finish(stage_ref, out_hbm, sem):
    for i in range(PARTS):
        send_part(stage_ref, out_hbm, sem, i).wait()


def build_z(zb_ref, zf_ref):
    channel = (lax.broadcasted_iota(jnp.int32, (2 * NZ, 256), 1) // 8) % 4
    for group in range(2):
        table = zb_ref[:, group * 256 : (group + 1) * 256].astype(F32)
        for c in range(4):
            row = group * 1024 + c * 256
            zf_ref[row : row + 256, :] = jnp.where(channel == c, table, 0.0).astype(BF16)


def low_lanes(rows):
    return lax.broadcasted_iota(jnp.int32, (rows, 128), 1) % 64 < 32


def z_forward(planes_ref, zf_ref, wide_ref, stage_ref, out_hbm, sem):
    low = low_lanes(256)
    for half in range(2):
        first, second = (
            dot(
                planes_ref[half * 256 : (half + 1) * 256, group * 1024 : (group + 1) * 1024],
                zf_ref[group * 1024 : (group + 1) * 1024, :],
            )
            for group in range(2)
        )
        for t in range(2):
            one, two = first[:, t * 128 : (t + 1) * 128], second[:, t * 128 : (t + 1) * 128]
            for j, value in enumerate((jnp.where(low, one, two), jnp.where(low, two, one))):
                for x in range(X):
                    wide_ref[pl.ds((2 * t + j) * 16 + half * 8 + x, 32, stride=64), :] = value[
                        x * 32 : (x + 1) * 32
                    ]
    for i in range(PARTS):
        rows = 128 // PARTS
        stage_ref[i * rows : (i + 1) * rows] = (
            wide_ref[i * rows * 16 : (i + 1) * rows * 16, :].astype(BF16).reshape(rows, 16, 128)
        )
        send_part(stage_ref, out_hbm, sem, i).start()


def z_inverse(in_ref, zf_ref, wide_ref, gather_ref, rolled_ref):
    rows = in_ref.shape[1]
    wide_ref[...] = in_ref[...].astype(F32).reshape(128 * rows, 128)
    low = low_lanes(32)
    for half in range(2):
        for x in range(X):
            row = (half * 8 + x) * 32
            for t in range(2):
                even, odd = (
                    wide_ref[pl.ds((2 * t + j) * rows + half * 8 + x, 32, stride=4 * rows), :]
                    for j in range(2)
                )
                for group, value in enumerate((jnp.where(low, even, odd), jnp.where(low, odd, even))):
                    column = group * 256 + t * 128
                    gather_ref[row : row + 32, column : column + 128] = value.astype(BF16)
    for c in range(8):
        group = c // 4
        rolled_ref[:, c * 256 : (c + 1) * 256] = dot_nt(
            gather_ref[:, group * 256 : (group + 1) * 256], zf_ref[c * 256 : (c + 1) * 256, :]
        ).astype(BF16)


def y_forward(ty_ref, pair, planes_ref, x, op):
    result = dot(ty_ref[...], pair)
    half, first = op // 4, (op % 4) * 2
    row = half * 256 + x * 32
    rows = pl.ds(row if isinstance(x, int) else pl.multiple_of(row, 32), 32)
    for j in range(2):
        for part in range(2):
            column = (first + j) * 256 + part * 128
            planes_ref[rows, column : column + 128] = result[
                part * 32 : (part + 1) * 32, j * 128 : (j + 1) * 128
            ].astype(BF16)
    return result


def y_inverse(tyt_ref, rolled_ref, x, op):
    half, first = op // 4, (op % 4) * 2
    rows = pl.ds(pl.multiple_of(half * 256 + x * 32, 32), 32)
    blocks = []
    for j in range(2):
        column = (first + j) * 256
        blocks.append(
            jnp.concatenate(
                [
                    rolled_ref[rows, column : column + 128],
                    rolled_ref[rows, column + 128 : column + 256],
                ],
                axis=0,
            )
        )
    return dot(tyt_ref[...], jnp.concatenate(blocks, axis=1))


class Planes:
    def __init__(self, hbm_ref, vmem_ref, sem, given, out=False):
        self.hbm_ref, self.vmem_ref, self.sem, self.given, self.out = hbm_ref, vmem_ref, sem, given, out

    def copy(self, x, channels):
        far = self.hbm_ref.at[0, channels, x] if self.given else self.hbm_ref.at[x, channels]
        near = self.vmem_ref.at[x, channels]
        source, target = (near, far) if self.out else (far, near)
        return pltpu.make_async_copy(source, target, self.sem.at[x])

    def start(self, x):
        for c in range(0, C, CUT):
            self.copy(x, pl.ds(c, CUT)).start()

    def wait(self, x):
        self.copy(x, pl.ds(0, C)).wait()


def field_kernel(
    field_hbm, ty_hbm, zb_hbm, out_hbm,
    zf_ref, planes_ref, wide_ref, field_ref, ty_ref, zb_ref, stage_ref, sem, ty_sem, zb_sem, sent_sem,
):
    load = Planes(field_hbm, field_ref, sem, True)
    load_ty = pltpu.make_async_copy(ty_hbm, ty_ref, ty_sem)
    load_zb = pltpu.make_async_copy(zb_hbm, zb_ref, zb_sem)
    load_ty.start()
    load.start(0)
    load_zb.start()
    for x in range(1, AHEAD):
        load.start(x)
    load_ty.wait()
    load_zb.wait()
    build_z(zb_ref, zf_ref)
    for x in range(X):
        if x + AHEAD < X:
            load.start(x + AHEAD)
        load.wait(x)
        for op in range(8):
            pair = jnp.concatenate([field_ref[x, 2 * op], field_ref[x, 2 * op + 1]], axis=1)
            y_forward(ty_ref, pair, planes_ref, x, op)
    z_forward(planes_ref, zf_ref, wide_ref, stage_ref, out_hbm, sent_sem)
    finish(stage_ref, out_hbm, sent_sem)


def y_blocks(ref, x):
    return jnp.concatenate(
        [ref[x, :, b * 16 : (b + 1) * 16, :].reshape(256, 128) for b in range(16)], axis=1
    )


def owner_rows():
    group = lax.broadcasted_iota(jnp.int32, (256, 16), 0) // 16
    return jnp.where(group == lax.broadcasted_iota(jnp.int32, (256, 16), 1), 1.0, 0.0)


def same_row(value):
    row = lax.broadcasted_iota(jnp.int32, (256, 256), 0) % 16
    column = lax.broadcasted_iota(jnp.int32, (256, 256), 1) % 16
    return jnp.where(row == column, value, 0.0)


def map_planes(scale, in_hbm, map_rows, bias, out_hbm, in_ref, out_ref, in_sem, out_sem):
    load = Planes(in_hbm, in_ref, in_sem, len(in_hbm.shape) == 5)
    store = Planes(out_hbm, out_ref, out_sem, False, True)
    for x in range(X):
        load.start(x)
    kron = same_row(dot_nt(map_rows.astype(BF16), owner_rows().astype(BF16))).astype(BF16)

    def step(x, _):
        load.wait(x)
        for b in range(8):
            pair = jnp.concatenate(
                [in_ref[x, :, y : y + 16, :].reshape(256, 128) for y in (b * 32, b * 32 + 16)],
                axis=1,
            )
            result = dot(kron, pair)
            if bias is not None:
                result = result + bias
            result = (result * scale).astype(BF16)
            for j in range(2):
                y = b * 32 + j * 16
                out_ref[x, :, y : y + 16, :] = result[:, j * 128 : (j + 1) * 128].reshape(C, 16, 128)
        store.start(x)
        return 0

    lax.fori_loop(0, X, step, 0)
    for x in range(X):
        store.wait(x)


def pre_kernel(in_hbm, weight_ref, bias_ref, out_hbm, in_ref, out_ref, in_sem, out_sem):
    map_rows = dot_nt(owner_rows().astype(BF16), weight_ref[...])
    bias = jnp.sum(owner_rows() * bias_ref[...], axis=1, keepdims=True)
    map_planes(GK, in_hbm, map_rows, bias, out_hbm, in_ref, out_ref, in_sem, out_sem)


def back_kernel(in_hbm, weight_ref, out_hbm, in_ref, out_ref, in_sem, out_sem):
    map_rows = dot(owner_rows().astype(BF16), weight_ref[...])
    map_planes(0.5, in_hbm, map_rows, None, out_hbm, in_ref, out_ref, in_sem, out_sem)


def slope_of(h):
    one, add = BF16(1.0), BF16(GA)
    square = h * h
    t = jnp.tanh(h * (square + add))
    slope = h * (square * BF16(3.0) + add)
    return (one + t) * (one + (one - t) * slope)


def signal_kernel(
    in_ref, pre_hbm, cot_hbm, ty_ref, tyt_ref, zb_ref,
    dpre_hbm, out_hbm, bias_ref,
    zf_ref, planes_ref, wide_ref, gather_ref, rolled_ref, pre_ref, cot_ref, stage_ref,
    pre_sem, cot_sem, out_sem, sent_sem,
):
    load_pre = Planes(pre_hbm, pre_ref, pre_sem, False)
    load_cot = Planes(cot_hbm, cot_ref, cot_sem, True)
    store = Planes(dpre_hbm, cot_ref, out_sem, False, True)
    for x in range(X):
        load_pre.start(x)
        load_cot.start(x)
    build_z(zb_ref, zf_ref)
    z_inverse(in_ref, zf_ref, wide_ref, gather_ref, rolled_ref)
    bias_ref[...] = jnp.zeros_like(bias_ref)

    def step(x, _):
        load_pre.wait(x)
        load_cot.wait(x)
        for op in range(8):
            back = y_inverse(tyt_ref, rolled_ref, x, op)
            for j in range(2):
                o = 2 * op + j
                h = back[:, j * 128 : (j + 1) * 128].astype(BF16) + pre_ref[x, o]
                cot_ref[x, o] = slope_of(h) * cot_ref[x, o]
        store.start(x)
        for op in range(8):
            pair = jnp.concatenate([cot_ref[x, 2 * op], cot_ref[x, 2 * op + 1]], axis=1)
            result = y_forward(ty_ref, pair, planes_ref, x, op)
            bias_ref[op : op + 1, :] += result[0:1, :]
        return 0

    lax.fori_loop(0, X, step, 0)
    z_forward(planes_ref, zf_ref, wide_ref, stage_ref, out_hbm, sent_sem)
    for x in range(X):
        store.wait(x)
    finish(stage_ref, out_hbm, sent_sem)


def final_kernel(
    in_ref, mapped_hbm, tyt_ref, zb_ref, out_hbm, point_ref, bias_ref,
    zf_ref, wide_ref, gather_ref, rolled_ref, mapped_ref, out_ref, in_sem, out_sem,
):
    load = Planes(mapped_hbm, mapped_ref, in_sem, False)
    store = Planes(out_hbm, out_ref, out_sem, True, True)
    for x in range(X):
        load.start(x)
    build_z(zb_ref, zf_ref)
    z_inverse(in_ref, zf_ref, wide_ref, gather_ref, rolled_ref)

    def step(x, _):
        load.wait(x)
        for op in range(8):
            back = y_inverse(tyt_ref, rolled_ref, x, op)
            for j in range(2):
                o = 2 * op + j
                mapped = mapped_ref[x, o].astype(F32)
                out_ref[x, o] = (back[:, j * 128 : (j + 1) * 128] + mapped).astype(BF16)
        store.start(x)
        return 0

    lax.fori_loop(0, X, step, 0)
    total = jnp.sum(wide_ref[...].reshape(128, 24, 128)[:, 16:24, :], axis=0) * (0.5 * SCALE_P)
    lane = lax.broadcasted_iota(jnp.int32, (16, 128), 1)
    row = lax.broadcasted_iota(jnp.int32, (16, 128), 0)
    point = jnp.where(row < 8, total[0:1] + total[2:3], total[1:2] + total[3:4])
    point = jnp.where(lane // 16 == row % 8, point, 0.0)
    bias = jnp.where(lane < 32, total[4:5], 0.0)
    fold = lax.broadcasted_iota(jnp.int32, (128, 16), 0) % 16
    fold = jnp.where(fold == lax.broadcasted_iota(jnp.int32, (128, 16), 1), 1.0, 0.0)
    exact = lax.Precision.HIGHEST
    point_ref[...] = jnp.dot(point, fold, preferred_element_type=F32, precision=exact)
    bias_ref[...] = jnp.dot(bias, fold, preferred_element_type=F32, precision=exact)[0:1]
    for x in range(X):
        store.wait(x)


def swapped(which, w):
    return which + w * (1 - 2 * which)


def x_forward(which, in_ref, tx_ref, scale, modes_ref):
    data = jnp.concatenate([in_ref[:, b].reshape(1024, 128) for b in range(2)], axis=1)
    raw = dot(tx_ref[...], data)
    lane = lax.broadcasted_iota(jnp.int32, (128, 128), 1)
    sign = jnp.where(lane < 64, scale, -scale)
    for half in range(2):
        for b in range(2):
            cosine = raw[half * 256 : half * 256 + 128, b * 128 : (b + 1) * 128]
            sine = raw[half * 256 + 128 : half * 256 + 256, b * 128 : (b + 1) * 128]
            modes = cosine * scale + pltpu.roll(sine, 64, 1) * sign
            turned = modes.T
            for s in range(2):
                for w in range(2):
                    row = (half * 2 + b) * 128 + s * 64 + swapped(which, w) * 32
                    place = s * 64 + w * 32
                    modes_ref[pl.ds(pl.multiple_of(row, 32), 32), :] = turned[place : place + 32]


def x_inverse(mixed, txi_ref, stage_ref, extra, send):
    lane = lax.broadcasted_iota(jnp.int32, (32, 128), 1)
    rows = []
    for half in range(2):
        turned = [mixed(half, b).T[:32] for b in range(2)]
        rows.append(jnp.concatenate(turned, axis=1))
        rows.append(
            jnp.concatenate(
                [jnp.where(lane < 64, -1.0, 1.0) * pltpu.roll(g, 64, 1) for g in turned], axis=1
            )
        )
    right = jnp.concatenate(rows, axis=0).astype(BF16)
    parts = 1 if send is None else PARTS
    count = SLABS // parts
    for i in range(parts):
        result = dot(txi_ref[i * count * 16 : (i + 1) * count * 16, :], right)
        if extra is None:
            result = result.astype(BF16)
        for b in range(2):
            block = result[:, b * 128 : (b + 1) * 128].reshape(count, 16, 128)
            if extra is not None:
                more = jnp.broadcast_to(extra[None], (count, 8, 128))
                block = jnp.concatenate([block, more], axis=1).astype(BF16)
            stage_ref[i * count : (i + 1) * count, b] = block
        if send is not None:
            send_part(stage_ref, *send, i).start()


def mix_kernel(which_ref, in_ref, weight_ref, tx_ref, txi_ref, out_ref, modes_ref, mixed_ref):
    which = which_ref[0]
    x_forward(which, in_ref, tx_ref, SCALE_F, modes_ref)
    first = which * 8
    for p in range(8):
        real = weight_ref[first + p, 0].astype(F32)
        imag = weight_ref[first + p, 1].astype(F32)
        for b in range(2):
            u = [
                [modes_ref[pl.ds((half * 2 + b) * 128 + s * 64 + p, 8, stride=8), :] for s in range(2)]
                for half in range(2)
            ]
            for q in range(4):
                total = [0.0, 0.0]
                for half in range(2):
                    w0 = real[half * 8 : half * 8 + 8, q * 128 : (q + 1) * 128]
                    w1 = imag[half * 8 : half * 8 + 8, q * 128 : (q + 1) * 128]
                    u0, u1 = u[half]
                    total[0] = total[0] + (u0 * w0 - u1 * w1)
                    total[1] = total[1] + (u0 * w1 + u1 * w0)
                for s in range(2):
                    row = (b * 2 + s) * 8 + p
                    mixed_ref[row : row + 1, q * 128 : (q + 1) * 128] = jnp.sum(
                        total[s], axis=0, keepdims=True
                    ) * (SCALE_I * GK)

    def mixed(half, b):
        pieces = []
        for s in range(2):
            row = (b * 2 + s) * 8
            for w in range(2):
                column = pl.multiple_of((half * 2 + swapped(which, w)) * 128, 128)
                piece = mixed_ref[row : row + 8, pl.ds(column, 128)]
                for r in range(4):
                    pieces.append(pltpu.roll(piece, 128 - 32 * r, 1) if r else piece)
        return jnp.concatenate(pieces, axis=0)

    x_inverse(mixed, txi_ref, out_ref, None, None)


def adjoint_kernel(
    which_ref, in_ref, weight_ref, tx_ref, txi_ref, extra_ref,
    out_hbm, rows_ref, short_ref, modes_ref, mixed_ref, stage_ref, sent_sem,
):
    which = which_ref[0]
    x_forward(which, in_ref, tx_ref, 0.5 * SCALE_I, modes_ref)
    group = lax.broadcasted_iota(jnp.int32, (8, 128), 1) // 32
    for b in range(2):
        for s in range(2):
            for q in range(4):
                half, c = q // 2, (q % 2) * 4
                row = (half * 2 + b) * 128 + s * 64 + c * 8
                value = modes_ref[row : row + 8, :]
                for r in range(1, 4):
                    value = jnp.where(group == r, modes_ref[row + 8 * r : row + 8 * r + 8, :], value)
                row = (b * 2 + s) * 8
                rows_ref[row : row + 8, q * 128 : (q + 1) * 128] = value
    first = which * 8
    for p in range(8):
        real = weight_ref[first + p, 0].astype(F32)
        imag = weight_ref[first + p, 1].astype(F32)
        for b in range(2):
            d0 = rows_ref[b * 16 + p : b * 16 + p + 1, :]
            d1 = rows_ref[b * 16 + 8 + p : b * 16 + 8 + p + 1, :]
            total0 = real * d0 + imag * d1
            total1 = real * d1 - imag * d0
            for s, total in enumerate((total0, total1)):
                folded = sum(total[:, q * 128 : (q + 1) * 128] for q in range(4))
                folded = folded + pltpu.roll(folded, 64, 1)
                folded = folded + pltpu.roll(folded, 32, 1)
                for half in range(2):
                    mixed_ref[pl.ds((half * 2 + b) * 128 + s * 64 + p, 8, stride=8), :] = (
                        folded[half * 8 : half * 8 + 8] * SCALE_F
                    )

    def mixed(half, b):
        pieces = []
        for s in range(2):
            for w in range(2):
                row = (half * 2 + b) * 128 + s * 64 + swapped(which, w) * 32
                pieces.append(mixed_ref[pl.ds(pl.multiple_of(row, 32), 32), :])
        return jnp.concatenate(pieces, axis=0)

    x_inverse(mixed, txi_ref, stage_ref, extra_ref[...], (out_hbm, sent_sem))
    short_ref[...] = rows_ref[...].astype(BF16)
    finish(stage_ref, out_hbm, sent_sem)


def spec_kernel(which_ref, u_ref, v_bf_ref, d_ref, e_bf_ref, out_ref, v_ref, e_ref):
    group = lax.broadcasted_iota(jnp.int32, (128, 128), 1) // 32
    short = v_bf_ref[...].astype(F32)
    for i in range(4):
        part = jnp.where(group == i, short, 0.0)
        part = part + pltpu.roll(part, 32, 1)
        v_ref[i * 128 : (i + 1) * 128, :] = part + pltpu.roll(part, 64, 1)
    e_ref[...] = e_bf_ref[...].astype(F32)
    mine = which_ref[0] * 8
    other = 8 - mine
    for start, modes_ref, rows_ref in ((mine, u_ref, d_ref), (other, v_ref, e_ref)):
        for p in range(8):
            for half in range(2):
                u = [
                    [
                        modes_ref[pl.ds((half * 2 + b) * 128 + s * 64 + p, 8, stride=8), :] * SCALE_W
                        for s in range(2)
                    ]
                    for b in range(2)
                ]
                for q in range(4):
                    real = imag = 0.0
                    for b in range(2):
                        d0 = rows_ref[b * 16 + p : b * 16 + p + 1, q * 128 : (q + 1) * 128]
                        d1 = rows_ref[b * 16 + 8 + p : b * 16 + 9 + p, q * 128 : (q + 1) * 128]
                        real = real + (u[b][0] * d0 + u[b][1] * d1)
                        imag = imag + (u[b][0] * d1 - u[b][1] * d0)
                    lanes = slice(q * 128, (q + 1) * 128)
                    out_ref[start + p, 0, half * 8 : half * 8 + 8, lanes] = real
                    out_ref[start + p, 1, half * 8 : half * 8 + 8, lanes] = imag


def point_kernel(
    field_hbm, dpre_hbm, bias_ref, modes_ref, out_ref, short_ref,
    acc_ref, field_ref, dpre_ref, field_sem, dpre_sem,
):
    load_field = Planes(field_hbm, field_ref, field_sem, True)
    load_dpre = Planes(dpre_hbm, dpre_ref, dpre_sem, False)
    for x in range(X):
        load_field.start(x)
        load_dpre.start(x)
    group = lax.broadcasted_iota(jnp.int32, (128, 128), 1) // 32
    short = modes_ref[0:128, :]
    for i in range(1, 4):
        short = jnp.where(group == i, modes_ref[i * 128 : (i + 1) * 128, :], short)
    short_ref[...] = short.astype(BF16)
    acc_ref[...] = jnp.zeros_like(acc_ref)

    def step(x, _):
        load_field.wait(x)
        load_dpre.wait(x)
        acc_ref[...] += dot_nt(y_blocks(field_ref, x), y_blocks(dpre_ref, x))
        return 0

    lax.fori_loop(0, X, step, 0)
    kept = same_row(acc_ref[...])
    rows = jnp.concatenate(
        [jnp.sum(kept[i * 16 : (i + 1) * 16], axis=0, keepdims=True) for i in range(16)], axis=0
    )
    owner = lax.broadcasted_iota(jnp.int32, (256, 128), 0) // 16
    column = lax.broadcasted_iota(jnp.int32, (256, 128), 1) % 16
    point = jnp.dot(
        rows,
        jnp.where(owner == column, 1.0, 0.0),
        preferred_element_type=F32,
        precision=lax.Precision.HIGHEST,
    )
    lane = lax.broadcasted_iota(jnp.int32, (8, 128), 1)
    row = lax.broadcasted_iota(jnp.int32, (8, 128), 0)
    first, second = (
        jnp.sum(jnp.where(lane // 16 == row, point[h * 8 : h * 8 + 8], 0.0), axis=0, keepdims=True)
        for h in range(2)
    )
    even = jnp.sum(bias_ref[:, 0:128], axis=1, keepdims=True)
    odd = jnp.sum(bias_ref[:, 128:256], axis=1, keepdims=True)
    bias = jnp.where(lane == 2 * row, even, jnp.where(lane == 2 * row + 1, odd, 0.0))
    bias = jnp.sum(bias, axis=0, keepdims=True)
    value = jnp.where(
        (row == 0) | (row == 2), first, jnp.where((row == 1) | (row == 3), second, 0.0)
    )
    value = jnp.where(row == 4, bias, value)
    high = value.astype(BF16).astype(F32)
    low = value - high
    packed = jnp.where(row < 2, high, jnp.where(row < 4, low, 0.0))
    packed = jnp.where((row == 4) & (lane < 16), high, packed)
    out_ref[...] = jnp.where((row == 4) & (lane >= 16), pltpu.roll(low, 16, 1), packed)


SMEM = pl.BlockSpec(memory_space=pltpu.SMEM)
VMEM = pl.BlockSpec(memory_space=pltpu.VMEM)
HBM = pl.BlockSpec(memory_space=pltpu.HBM)
BUFFER = (128, 16, 128)
PLANES = (X, C, NY, NZ)
GIVEN = (1, C, X, NY, NZ)


def struct(shape, dtype):
    return jax.ShapeDtypeStruct(shape, dtype)


def call(kernel, out_shape, in_specs, out_specs, scratch, flops, moved, limit, name):
    return pl.pallas_call(
        kernel,
        out_shape=out_shape,
        in_specs=in_specs,
        out_specs=out_specs,
        scratch_shapes=scratch,
        compiler_params=pltpu.CompilerParams(vmem_limit_bytes=limit * MIB),
        cost_estimate=pl.CostEstimate(flops=flops, bytes_accessed=moved, transcendentals=0),
        name=name,
    )


def exchange(buffer):
    return lax.all_to_all(buffer, BOTH, 0, 0, tiled=True)


def grouped(buffer):
    return buffer.reshape((SLABS, 2) + buffer.shape[1:])


def flat(buffer):
    return buffer.reshape((128,) + buffer.shape[2:])


def body(field, cotangent, spectral_weight, point_weight, point_bias):
    ty, tyt, zb, tx, txi = (jnp.asarray(t) for t in tables())
    which = lax.axis_index("batch").astype(jnp.int32).reshape(1)
    zf = pltpu.VMEM((2048, 256), BF16)
    planes = pltpu.VMEM((512, 2048), BF16)
    wide = pltpu.VMEM((2048, 128), F32)
    gather = pltpu.VMEM((512, 512), BF16)
    held = pltpu.VMEM(PLANES, BF16)
    stage = pltpu.VMEM(BUFFER, BF16)
    sems = pltpu.SemaphoreType.DMA((X,))
    big = 8 * MIB
    swap = [(0, 1), (1, 0)]

    sent = call(
        field_kernel, struct(BUFFER, BF16), [HBM, HBM, HBM], HBM,
        [zf, planes, wide, held, pltpu.VMEM((64, NY), BF16), pltpu.VMEM((256, 512), BF16), stage,
         sems, pltpu.SemaphoreType.DMA, pltpu.SemaphoreType.DMA, sems], 2 * 10**9, big, 60, "field_planes",
    )(field, ty, zb)
    got = exchange(sent)
    pre = call(
        pre_kernel, struct(PLANES, BF16), [HBM, VMEM, VMEM], HBM,
        [held, held, sems, sems], 2 * 10**9, 2 * big, LIMIT, "point_map",
    )(field, point_weight, point_bias.reshape(1, C))
    got, pre = lax.optimization_barrier((got, pre))
    back, modes_u = call(
        mix_kernel,
        (struct((SLABS, 2, 16, 128), BF16), struct((512, 128), F32)),
        [SMEM] + [VMEM] * 4, (VMEM, VMEM),
        [pltpu.VMEM((32, 512), F32)],
        10**9, 3 * MIB, 32, "mix_modes",
    )(which, grouped(got), spectral_weight, tx, txi)
    got = exchange(flat(back))
    dpre, sent, bias_rows = call(
        signal_kernel,
        (struct(PLANES, BF16), struct(BUFFER, BF16), struct((8, 256), F32)),
        [VMEM, HBM, HBM, VMEM, VMEM, VMEM], (HBM, HBM, VMEM),
        [zf, planes, wide, gather, planes, held, held, stage, sems, sems, sems, sems],
        6 * 10**9, 3 * big, LIMIT, "signal",
    )(got, pre, cotangent, ty, tyt, zb)
    got = exchange(sent)
    extra, short_u = call(
        point_kernel, (struct((8, 128), F32), struct((128, 128), BF16)),
        [HBM, HBM, VMEM, VMEM], (VMEM, VMEM),
        [pltpu.VMEM((256, 256), F32), held, held, sems, sems],
        2 * 10**9, 2 * big, LIMIT, "point_gradient",
    )(field, dpre, bias_rows, modes_u)
    back, rows_d, short_d = call(
        adjoint_kernel,
        (struct((SLABS, 2, 24, 128), BF16), struct((32, 512), F32), struct((32, 512), BF16)),
        [SMEM] + [VMEM] * 5, (HBM, VMEM, VMEM),
        [pltpu.VMEM((512, 128), F32), pltpu.VMEM((512, 128), F32),
         pltpu.VMEM((SLABS, 2, 24, 128), BF16), sems],
        10**9, 3 * MIB, 32, "adjoint_modes",
    )(which, grouped(got), spectral_weight, tx, txi, extra)
    dpre, short_d, short_u = lax.optimization_barrier((dpre, short_d, short_u))
    got = exchange(flat(back))
    other_u = lax.ppermute(short_u, "batch", swap)
    other_d = lax.ppermute(short_d, "batch", swap)
    mapped = call(
        back_kernel, struct(PLANES, BF16), [HBM, VMEM], HBM,
        [held, held, sems, sems], 2 * 10**9, 2 * big, LIMIT, "point_map_back",
    )(dpre, point_weight)
    grad_spec = call(
        spec_kernel, struct((16, 2, C, 512), F32), [SMEM] + [VMEM] * 4, VMEM,
        [pltpu.VMEM((512, 128), F32), pltpu.VMEM((32, 512), F32)],
        10**7, 2 * MIB, 32, "spectral_gradient",
    )(which, modes_u, other_u, rows_d, other_d)
    input_grad, grad_point, grad_bias = call(
        final_kernel, (struct(GIVEN, BF16), struct((C, C), F32), struct((1, C), F32)),
        [VMEM, HBM, VMEM, VMEM], (HBM, VMEM, VMEM),
        [zf, pltpu.VMEM((3072, 128), F32), gather, planes, held, held, sems, sems],
        4 * 10**9, 2 * big, LIMIT, "input_gradient",
    )(got, mapped, tyt, zb)
    return input_grad, grad_spec, grad_point, grad_bias.reshape(C)


def solution(mesh):
    planes = P("batch", None, "slab", None, None)
    return jax.shard_map(
        body,
        mesh=mesh,
        in_specs=(planes, planes, P("slab", None, None, None), P(), P()),
        out_specs=(planes, P("slab", None, None, None), P(), P()),
        check_vma=False,
    )
```

```python
import math

import jax
import jax.numpy as jnp
import numpy as np
from jax import lax
from jax.experimental import pallas as pl
from jax.experimental.pallas import tpu as pltpu
from jax.sharding import PartitionSpec as P

C = 16
X = 8
NY = 256
NZ = 128
NX = 512
MODES = 32
SLABS = 64
CELLS = NX * NY * NZ
SCALE_F = 1.0 / math.sqrt(CELLS)
SCALE_I = 1.0 / math.sqrt(MODES**3)
SCALE_P = 1.0 / math.sqrt(2 * CELLS)
SCALE_W = math.sqrt(MODES**3 / (2 * CELLS))
GELU_A = math.sqrt(2.0 / math.pi)
GK = (GELU_A * 0.044715) ** (1.0 / 3.0)
GA = GELU_A / GK
BOTH = ("slab", "batch")
F32 = jnp.float32
BF16 = jnp.bfloat16
MIB = 1 << 20
LIMIT = 48
CUT = 8
AHEAD = 4
Z_CUTS = (4, 8)
PARTS = 8


def freqs(number, length):
    index = np.arange(number)
    return np.where(index < number // 2, index, index + length - number)


def angles(length, frequencies):
    product = (np.arange(length)[:, None] * frequencies[None, :]) % length
    return product * (2.0 * math.pi / length)


def tables():
    thy = angles(NY, freqs(MODES, NY))
    thz = angles(NZ, np.arange(MODES))
    thx = angles(NX, freqs(MODES, NX))
    ty = np.concatenate([np.cos(thy).T, -np.sin(thy).T], axis=0)
    cos, sin = np.cos(thz), np.sin(thz)
    rot = np.zeros((2, NZ, 2, MODES))
    rot[0, :, 0], rot[1, :, 0] = cos, sin
    rot[1, :, 1], rot[0, :, 1] = cos, -sin
    zb = rot.reshape(2, NZ, 2, 2, 2, 8).transpose(0, 1, 3, 2, 4, 5)
    zb = np.stack([zb, zb[:, :, :, :, ::-1]], axis=2)[:, :, :, :, :, :, None, :]
    zb = np.broadcast_to(zb, (2, NZ, 2, 2, 2, 2, 4, 8)).reshape(2 * NZ, 512)
    cs = np.stack([np.cos(thx), np.sin(thx)]).reshape(2, SLABS, X, MODES)
    tx = np.zeros((2, 2, 4, MODES, SLABS, 2, X))
    txi = np.zeros((SLABS, 2, X, 2, 2, MODES))
    for half in range(2):
        tx[half, :, :, :, :, half] = cs.transpose(0, 3, 1, 2)[:, None]
        txi[:, half, :, half] = cs.transpose(1, 2, 0, 3)
    return tuple(
        np.asarray(t, np.float32).astype(BF16)
        for t in (ty, ty.T, zb, tx.reshape(512, 1024), txi.reshape(1024, 128))
    )


def dot(left, right):
    return jnp.dot(left, right, preferred_element_type=F32)


def dot_nt(left, right):
    return lax.dot_general(left, right, (((1,), (1,)), ((), ())), preferred_element_type=F32)


def send_part(stage_ref, out_hbm, sem, i):
    count = out_hbm.shape[0] // PARTS
    part = pl.ds(i * count, count)
    return pltpu.make_async_copy(stage_ref.at[part], out_hbm.at[part], sem.at[i])


def finish(stage_ref, out_hbm, sem):
    for i in range(PARTS):
        send_part(stage_ref, out_hbm, sem, i).wait()


def build_z(zb_ref, zf_ref):
    channel = (lax.broadcasted_iota(jnp.int32, (2 * NZ, 256), 1) // 8) % 4
    for group in range(2):
        table = zb_ref[:, group * 256 : (group + 1) * 256].astype(F32)
        for c in range(4):
            row = group * 1024 + c * 256
            zf_ref[row : row + 256, :] = jnp.where(channel == c, table, 0.0).astype(BF16)


def low_lanes(rows):
    return lax.broadcasted_iota(jnp.int32, (rows, 128), 1) % 64 < 32


def z_part(planes_ref, zf_ref, wide_ref, start, count):
    low = low_lanes(count * 32)
    for half in range(2):
        row = half * 256 + start * 32
        first, second = (
            dot(
                planes_ref[row : row + count * 32, group * 1024 : (group + 1) * 1024],
                zf_ref[group * 1024 : (group + 1) * 1024, :],
            )
            for group in range(2)
        )
        for t in range(2):
            one, two = first[:, t * 128 : (t + 1) * 128], second[:, t * 128 : (t + 1) * 128]
            for j, value in enumerate((jnp.where(low, one, two), jnp.where(low, two, one))):
                for x in range(count):
                    place = (2 * t + j) * 16 + half * 8 + start + x
                    wide_ref[pl.ds(place, 32, stride=64), :] = value[x * 32 : (x + 1) * 32]


def z_send(wide_ref, stage_ref, out_hbm, sem):
    rows = 128 // PARTS
    for i in range(PARTS):
        stage_ref[i * rows : (i + 1) * rows] = (
            wide_ref[i * rows * 16 : (i + 1) * rows * 16, :].astype(BF16).reshape(rows, 16, 128)
        )
        send_part(stage_ref, out_hbm, sem, i).start()


def z_inverse(in_ref, zf_ref, wide_ref, gather_ref, rolled_ref):
    rows = in_ref.shape[1]
    wide_ref[...] = in_ref[...].astype(F32).reshape(128 * rows, 128)
    low = low_lanes(32)
    for half in range(2):
        for x in range(X):
            row = (half * 8 + x) * 32
            for t in range(2):
                even, odd = (
                    wide_ref[pl.ds((2 * t + j) * rows + half * 8 + x, 32, stride=4 * rows), :]
                    for j in range(2)
                )
                for group, value in enumerate((jnp.where(low, even, odd), jnp.where(low, odd, even))):
                    column = group * 256 + t * 128
                    gather_ref[row : row + 32, column : column + 128] = value.astype(BF16)
    for c in range(8):
        group = c // 4
        rolled_ref[:, c * 256 : (c + 1) * 256] = dot_nt(
            gather_ref[:, group * 256 : (group + 1) * 256], zf_ref[c * 256 : (c + 1) * 256, :]
        ).astype(BF16)


def y_forward(ty_ref, pair, planes_ref, x, op):
    result = dot(ty_ref[...], pair)
    half, first = op // 4, (op % 4) * 2
    row = half * 256 + x * 32
    rows = pl.ds(row if isinstance(x, int) else pl.multiple_of(row, 32), 32)
    for j in range(2):
        for part in range(2):
            column = (first + j) * 256 + part * 128
            planes_ref[rows, column : column + 128] = result[
                part * 32 : (part + 1) * 32, j * 128 : (j + 1) * 128
            ].astype(BF16)
    return result


def y_inverse(tyt_ref, rolled_ref, x, op):
    half, first = op // 4, (op % 4) * 2
    rows = pl.ds(pl.multiple_of(half * 256 + x * 32, 32), 32)
    blocks = []
    for j in range(2):
        column = (first + j) * 256
        blocks.append(
            jnp.concatenate(
                [
                    rolled_ref[rows, column : column + 128],
                    rolled_ref[rows, column + 128 : column + 256],
                ],
                axis=0,
            )
        )
    return dot(tyt_ref[...], jnp.concatenate(blocks, axis=1))


class Planes:
    def __init__(self, hbm_ref, vmem_ref, sem, given, out=False):
        self.hbm_ref, self.vmem_ref, self.sem, self.given, self.out = hbm_ref, vmem_ref, sem, given, out

    def copy(self, x, channels):
        far = self.hbm_ref.at[0, channels, x] if self.given else self.hbm_ref.at[x, channels]
        near = self.vmem_ref.at[x, channels]
        source, target = (near, far) if self.out else (far, near)
        return pltpu.make_async_copy(source, target, self.sem.at[x])

    def start(self, x):
        for c in range(0, C, CUT):
            self.copy(x, pl.ds(c, CUT)).start()

    def wait(self, x):
        self.copy(x, pl.ds(0, C)).wait()


def field_kernel(
    field_hbm, ty_hbm, zb_hbm, out_hbm,
    zf_ref, planes_ref, wide_ref, field_ref, ty_ref, zb_ref, stage_ref, sem, ty_sem, zb_sem, sent_sem,
):
    load = Planes(field_hbm, field_ref, sem, True)
    load_ty = pltpu.make_async_copy(ty_hbm, ty_ref, ty_sem)
    load_zb = pltpu.make_async_copy(zb_hbm, zb_ref, zb_sem)
    load_ty.start()
    load.start(0)
    load_zb.start()
    for x in range(1, AHEAD):
        load.start(x)
    load_ty.wait()
    load_zb.wait()
    build_z(zb_ref, zf_ref)
    for x in range(X):
        if x + AHEAD < X:
            load.start(x + AHEAD)
        load.wait(x)
        for op in range(8):
            pair = jnp.concatenate([field_ref[x, 2 * op], field_ref[x, 2 * op + 1]], axis=1)
            y_forward(ty_ref, pair, planes_ref, x, op)
        if x + 1 in Z_CUTS:
            start = max([0] + [cut for cut in Z_CUTS if cut < x + 1])
            z_part(planes_ref, zf_ref, wide_ref, start, x + 1 - start)
    z_send(wide_ref, stage_ref, out_hbm, sent_sem)
    finish(stage_ref, out_hbm, sent_sem)


def y_blocks(ref, x):
    return jnp.concatenate(
        [ref[x, :, b * 16 : (b + 1) * 16, :].reshape(256, 128) for b in range(16)], axis=1
    )


def owner_rows():
    group = lax.broadcasted_iota(jnp.int32, (256, 16), 0) // 16
    return jnp.where(group == lax.broadcasted_iota(jnp.int32, (256, 16), 1), 1.0, 0.0)


def same_row(value):
    row = lax.broadcasted_iota(jnp.int32, (256, 256), 0) % 16
    column = lax.broadcasted_iota(jnp.int32, (256, 256), 1) % 16
    return jnp.where(row == column, value, 0.0)


def map_planes(scale, in_hbm, map_rows, bias, out_hbm, in_ref, out_ref, in_sem, out_sem):
    load = Planes(in_hbm, in_ref, in_sem, len(in_hbm.shape) == 5)
    store = Planes(out_hbm, out_ref, out_sem, False, True)
    for x in range(X):
        load.start(x)
    kron = same_row(dot_nt(map_rows.astype(BF16), owner_rows().astype(BF16))).astype(BF16)

    def step(x, _):
        load.wait(x)
        for b in range(8):
            pair = jnp.concatenate(
                [in_ref[x, :, y : y + 16, :].reshape(256, 128) for y in (b * 32, b * 32 + 16)],
                axis=1,
            )
            result = dot(kron, pair)
            if bias is not None:
                result = result + bias
            result = (result * scale).astype(BF16)
            for j in range(2):
                y = b * 32 + j * 16
                out_ref[x, :, y : y + 16, :] = result[:, j * 128 : (j + 1) * 128].reshape(C, 16, 128)
        store.start(x)
        return 0

    lax.fori_loop(0, X, step, 0)
    for x in range(X):
        store.wait(x)


def pre_kernel(in_hbm, weight_ref, bias_ref, out_hbm, in_ref, out_ref, in_sem, out_sem):
    map_rows = dot_nt(owner_rows().astype(BF16), weight_ref[...])
    bias = jnp.sum(owner_rows() * bias_ref[...], axis=1, keepdims=True)
    map_planes(GK, in_hbm, map_rows, bias, out_hbm, in_ref, out_ref, in_sem, out_sem)


def back_kernel(in_hbm, weight_ref, out_hbm, in_ref, out_ref, in_sem, out_sem):
    map_rows = dot(owner_rows().astype(BF16), weight_ref[...])
    map_planes(0.5, in_hbm, map_rows, None, out_hbm, in_ref, out_ref, in_sem, out_sem)


def slope_of(h):
    one, add = BF16(1.0), BF16(GA)
    square = h * h
    t = jnp.tanh(h * (square + add))
    slope = h * (square * BF16(3.0) + add)
    return (one + t) * (one + (one - t) * slope)


def signal_kernel(
    in_ref, pre_hbm, cot_hbm, ty_ref, tyt_ref, zb_ref,
    dpre_hbm, out_hbm, bias_ref,
    zf_ref, planes_ref, wide_ref, gather_ref, rolled_ref, pre_ref, cot_ref, stage_ref,
    pre_sem, cot_sem, out_sem, sent_sem,
):
    load_pre = Planes(pre_hbm, pre_ref, pre_sem, False)
    load_cot = Planes(cot_hbm, cot_ref, cot_sem, True)
    store = Planes(dpre_hbm, cot_ref, out_sem, False, True)
    for x in range(X):
        load_pre.start(x)
        load_cot.start(x)
    build_z(zb_ref, zf_ref)
    z_inverse(in_ref, zf_ref, wide_ref, gather_ref, rolled_ref)
    bias_ref[...] = jnp.zeros_like(bias_ref)

    def step(x, _):
        load_pre.wait(x)
        load_cot.wait(x)
        for op in range(8):
            back = y_inverse(tyt_ref, rolled_ref, x, op)
            for j in range(2):
                o = 2 * op + j
                h = back[:, j * 128 : (j + 1) * 128].astype(BF16) + pre_ref[x, o]
                cot_ref[x, o] = slope_of(h) * cot_ref[x, o]
        store.start(x)
        for op in range(8):
            pair = jnp.concatenate([cot_ref[x, 2 * op], cot_ref[x, 2 * op + 1]], axis=1)
            result = y_forward(ty_ref, pair, planes_ref, x, op)
            bias_ref[op : op + 1, :] += result[0:1, :]
        return 0

    lax.fori_loop(0, X, step, 0)
    z_part(planes_ref, zf_ref, wide_ref, 0, X)
    z_send(wide_ref, stage_ref, out_hbm, sent_sem)
    for x in range(X):
        store.wait(x)
    finish(stage_ref, out_hbm, sent_sem)


def final_kernel(
    in_ref, mapped_hbm, tyt_ref, zb_ref, out_hbm, point_ref, bias_ref,
    zf_ref, wide_ref, gather_ref, rolled_ref, mapped_ref, out_ref, in_sem, out_sem,
):
    load = Planes(mapped_hbm, mapped_ref, in_sem, False)
    store = Planes(out_hbm, out_ref, out_sem, True, True)
    for x in range(X):
        load.start(x)
    build_z(zb_ref, zf_ref)
    z_inverse(in_ref, zf_ref, wide_ref, gather_ref, rolled_ref)

    def step(x, _):
        load.wait(x)
        for op in range(8):
            back = y_inverse(tyt_ref, rolled_ref, x, op)
            for j in range(2):
                o = 2 * op + j
                mapped = mapped_ref[x, o].astype(F32)
                out_ref[x, o] = (back[:, j * 128 : (j + 1) * 128] + mapped).astype(BF16)
        store.start(x)
        return 0

    lax.fori_loop(0, X, step, 0)
    total = jnp.sum(wide_ref[...].reshape(128, 24, 128)[:, 16:24, :], axis=0) * (0.5 * SCALE_P)
    lane = lax.broadcasted_iota(jnp.int32, (16, 128), 1)
    row = lax.broadcasted_iota(jnp.int32, (16, 128), 0)
    point = jnp.where(row < 8, total[0:1] + total[2:3], total[1:2] + total[3:4])
    point = jnp.where(lane // 16 == row % 8, point, 0.0)
    bias = jnp.where(lane < 32, total[4:5], 0.0)
    fold = lax.broadcasted_iota(jnp.int32, (128, 16), 0) % 16
    fold = jnp.where(fold == lax.broadcasted_iota(jnp.int32, (128, 16), 1), 1.0, 0.0)
    exact = lax.Precision.HIGHEST
    point_ref[...] = jnp.dot(point, fold, preferred_element_type=F32, precision=exact)
    bias_ref[...] = jnp.dot(bias, fold, preferred_element_type=F32, precision=exact)[0:1]
    for x in range(X):
        store.wait(x)


def swapped(which, w):
    return which + w * (1 - 2 * which)


def x_forward(which, in_ref, tx_ref, scale, modes_ref):
    data = jnp.concatenate([in_ref[:, b].reshape(1024, 128) for b in range(2)], axis=1)
    raw = dot(tx_ref[...], data)
    lane = lax.broadcasted_iota(jnp.int32, (128, 128), 1)
    sign = jnp.where(lane < 64, scale, -scale)
    for half in range(2):
        for b in range(2):
            cosine = raw[half * 256 : half * 256 + 128, b * 128 : (b + 1) * 128]
            sine = raw[half * 256 + 128 : half * 256 + 256, b * 128 : (b + 1) * 128]
            modes = cosine * scale + pltpu.roll(sine, 64, 1) * sign
            turned = modes.T
            for s in range(2):
                for w in range(2):
                    row = (half * 2 + b) * 128 + s * 64 + swapped(which, w) * 32
                    place = s * 64 + w * 32
                    modes_ref[pl.ds(pl.multiple_of(row, 32), 32), :] = turned[place : place + 32]


def x_inverse(mixed, txi_ref, stage_ref, extra, send):
    lane = lax.broadcasted_iota(jnp.int32, (32, 128), 1)
    rows = []
    for half in range(2):
        turned = [mixed(half, b).T[:32] for b in range(2)]
        rows.append(jnp.concatenate(turned, axis=1))
        rows.append(
            jnp.concatenate(
                [jnp.where(lane < 64, -1.0, 1.0) * pltpu.roll(g, 64, 1) for g in turned], axis=1
            )
        )
    right = jnp.concatenate(rows, axis=0).astype(BF16)
    parts = 1 if send is None else PARTS
    count = SLABS // parts
    for i in range(parts):
        result = dot(txi_ref[i * count * 16 : (i + 1) * count * 16, :], right)
        if extra is None:
            result = result.astype(BF16)
        for b in range(2):
            block = result[:, b * 128 : (b + 1) * 128].reshape(count, 16, 128)
            if extra is not None:
                more = jnp.broadcast_to(extra[None], (count, 8, 128))
                block = jnp.concatenate([block, more], axis=1).astype(BF16)
            stage_ref[i * count : (i + 1) * count, b] = block
        if send is not None:
            send_part(stage_ref, *send, i).start()


def mix_kernel(which_ref, in_ref, weight_ref, tx_ref, txi_ref, out_ref, modes_ref, mixed_ref):
    which = which_ref[0]
    x_forward(which, in_ref, tx_ref, SCALE_F, modes_ref)
    first = which * 8
    for p in range(8):
        real = weight_ref[first + p, 0].astype(F32)
        imag = weight_ref[first + p, 1].astype(F32)
        for b in range(2):
            u = [
                [modes_ref[pl.ds((half * 2 + b) * 128 + s * 64 + p, 8, stride=8), :] for s in range(2)]
                for half in range(2)
            ]
            for q in range(4):
                total = [0.0, 0.0]
                for half in range(2):
                    w0 = real[half * 8 : half * 8 + 8, q * 128 : (q + 1) * 128]
                    w1 = imag[half * 8 : half * 8 + 8, q * 128 : (q + 1) * 128]
                    u0, u1 = u[half]
                    total[0] = total[0] + (u0 * w0 - u1 * w1)
                    total[1] = total[1] + (u0 * w1 + u1 * w0)
                for s in range(2):
                    row = (b * 2 + s) * 8 + p
                    mixed_ref[row : row + 1, q * 128 : (q + 1) * 128] = jnp.sum(
                        total[s], axis=0, keepdims=True
                    ) * (SCALE_I * GK)

    def mixed(half, b):
        pieces = []
        for s in range(2):
            row = (b * 2 + s) * 8
            for w in range(2):
                column = pl.multiple_of((half * 2 + swapped(which, w)) * 128, 128)
                piece = mixed_ref[row : row + 8, pl.ds(column, 128)]
                for r in range(4):
                    pieces.append(pltpu.roll(piece, 128 - 32 * r, 1) if r else piece)
        return jnp.concatenate(pieces, axis=0)

    x_inverse(mixed, txi_ref, out_ref, None, None)


def adjoint_kernel(
    which_ref, in_ref, weight_ref, tx_ref, txi_ref, extra_ref,
    out_hbm, rows_ref, short_ref, modes_ref, mixed_ref, stage_ref, sent_sem,
):
    which = which_ref[0]
    x_forward(which, in_ref, tx_ref, 0.5 * SCALE_I, modes_ref)
    group = lax.broadcasted_iota(jnp.int32, (8, 128), 1) // 32
    for b in range(2):
        for s in range(2):
            for q in range(4):
                half, c = q // 2, (q % 2) * 4
                row = (half * 2 + b) * 128 + s * 64 + c * 8
                value = modes_ref[row : row + 8, :]
                for r in range(1, 4):
                    value = jnp.where(group == r, modes_ref[row + 8 * r : row + 8 * r + 8, :], value)
                row = (b * 2 + s) * 8
                rows_ref[row : row + 8, q * 128 : (q + 1) * 128] = value
    first = which * 8
    for p in range(8):
        real = weight_ref[first + p, 0].astype(F32)
        imag = weight_ref[first + p, 1].astype(F32)
        for b in range(2):
            d0 = rows_ref[b * 16 + p : b * 16 + p + 1, :]
            d1 = rows_ref[b * 16 + 8 + p : b * 16 + 8 + p + 1, :]
            total0 = real * d0 + imag * d1
            total1 = real * d1 - imag * d0
            for s, total in enumerate((total0, total1)):
                folded = sum(total[:, q * 128 : (q + 1) * 128] for q in range(4))
                folded = folded + pltpu.roll(folded, 64, 1)
                folded = folded + pltpu.roll(folded, 32, 1)
                for half in range(2):
                    mixed_ref[pl.ds((half * 2 + b) * 128 + s * 64 + p, 8, stride=8), :] = (
                        folded[half * 8 : half * 8 + 8] * SCALE_F
                    )

    def mixed(half, b):
        pieces = []
        for s in range(2):
            for w in range(2):
                row = (half * 2 + b) * 128 + s * 64 + swapped(which, w) * 32
                pieces.append(mixed_ref[pl.ds(pl.multiple_of(row, 32), 32), :])
        return jnp.concatenate(pieces, axis=0)

    x_inverse(mixed, txi_ref, stage_ref, extra_ref[...], (out_hbm, sent_sem))
    short_ref[...] = rows_ref[...].astype(BF16)
    finish(stage_ref, out_hbm, sent_sem)


def spec_kernel(which_ref, u_ref, v_bf_ref, d_ref, e_bf_ref, out_ref, v_ref, e_ref):
    group = lax.broadcasted_iota(jnp.int32, (128, 128), 1) // 32
    short = v_bf_ref[...].astype(F32)
    for i in range(4):
        part = jnp.where(group == i, short, 0.0)
        part = part + pltpu.roll(part, 32, 1)
        v_ref[i * 128 : (i + 1) * 128, :] = part + pltpu.roll(part, 64, 1)
    e_ref[...] = e_bf_ref[...].astype(F32)
    mine = which_ref[0] * 8
    other = 8 - mine
    for start, modes_ref, rows_ref in ((mine, u_ref, d_ref), (other, v_ref, e_ref)):
        for p in range(8):
            for half in range(2):
                u = [
                    [
                        modes_ref[pl.ds((half * 2 + b) * 128 + s * 64 + p, 8, stride=8), :] * SCALE_W
                        for s in range(2)
                    ]
                    for b in range(2)
                ]
                for q in range(4):
                    real = imag = 0.0
                    for b in range(2):
                        d0 = rows_ref[b * 16 + p : b * 16 + p + 1, q * 128 : (q + 1) * 128]
                        d1 = rows_ref[b * 16 + 8 + p : b * 16 + 9 + p, q * 128 : (q + 1) * 128]
                        real = real + (u[b][0] * d0 + u[b][1] * d1)
                        imag = imag + (u[b][0] * d1 - u[b][1] * d0)
                    lanes = slice(q * 128, (q + 1) * 128)
                    out_ref[start + p, 0, half * 8 : half * 8 + 8, lanes] = real
                    out_ref[start + p, 1, half * 8 : half * 8 + 8, lanes] = imag


def point_kernel(
    field_hbm, dpre_hbm, bias_ref, modes_ref, out_ref, short_ref,
    acc_ref, field_ref, dpre_ref, field_sem, dpre_sem,
):
    load_field = Planes(field_hbm, field_ref, field_sem, True)
    load_dpre = Planes(dpre_hbm, dpre_ref, dpre_sem, False)
    for x in range(X):
        load_field.start(x)
        load_dpre.start(x)
    group = lax.broadcasted_iota(jnp.int32, (128, 128), 1) // 32
    short = modes_ref[0:128, :]
    for i in range(1, 4):
        short = jnp.where(group == i, modes_ref[i * 128 : (i + 1) * 128, :], short)
    short_ref[...] = short.astype(BF16)
    acc_ref[...] = jnp.zeros_like(acc_ref)

    def step(x, _):
        load_field.wait(x)
        load_dpre.wait(x)
        acc_ref[...] += dot_nt(y_blocks(field_ref, x), y_blocks(dpre_ref, x))
        return 0

    lax.fori_loop(0, X, step, 0)
    kept = same_row(acc_ref[...])
    rows = jnp.concatenate(
        [jnp.sum(kept[i * 16 : (i + 1) * 16], axis=0, keepdims=True) for i in range(16)], axis=0
    )
    owner = lax.broadcasted_iota(jnp.int32, (256, 128), 0) // 16
    column = lax.broadcasted_iota(jnp.int32, (256, 128), 1) % 16
    point = jnp.dot(
        rows,
        jnp.where(owner == column, 1.0, 0.0),
        preferred_element_type=F32,
        precision=lax.Precision.HIGHEST,
    )
    lane = lax.broadcasted_iota(jnp.int32, (8, 128), 1)
    row = lax.broadcasted_iota(jnp.int32, (8, 128), 0)
    first, second = (
        jnp.sum(jnp.where(lane // 16 == row, point[h * 8 : h * 8 + 8], 0.0), axis=0, keepdims=True)
        for h in range(2)
    )
    even = jnp.sum(bias_ref[:, 0:128], axis=1, keepdims=True)
    odd = jnp.sum(bias_ref[:, 128:256], axis=1, keepdims=True)
    bias = jnp.where(lane == 2 * row, even, jnp.where(lane == 2 * row + 1, odd, 0.0))
    bias = jnp.sum(bias, axis=0, keepdims=True)
    value = jnp.where(
        (row == 0) | (row == 2), first, jnp.where((row == 1) | (row == 3), second, 0.0)
    )
    value = jnp.where(row == 4, bias, value)
    high = value.astype(BF16).astype(F32)
    low = value - high
    packed = jnp.where(row < 2, high, jnp.where(row < 4, low, 0.0))
    packed = jnp.where((row == 4) & (lane < 16), high, packed)
    out_ref[...] = jnp.where((row == 4) & (lane >= 16), pltpu.roll(low, 16, 1), packed)


SMEM = pl.BlockSpec(memory_space=pltpu.SMEM)
VMEM = pl.BlockSpec(memory_space=pltpu.VMEM)
HBM = pl.BlockSpec(memory_space=pltpu.HBM)
BUFFER = (128, 16, 128)
PLANES = (X, C, NY, NZ)
GIVEN = (1, C, X, NY, NZ)


def struct(shape, dtype):
    return jax.ShapeDtypeStruct(shape, dtype)


def call(kernel, out_shape, in_specs, out_specs, scratch, flops, moved, limit, name):
    return pl.pallas_call(
        kernel,
        out_shape=out_shape,
        in_specs=in_specs,
        out_specs=out_specs,
        scratch_shapes=scratch,
        compiler_params=pltpu.CompilerParams(vmem_limit_bytes=limit * MIB),
        cost_estimate=pl.CostEstimate(flops=flops, bytes_accessed=moved, transcendentals=0),
        name=name,
    )


def exchange(buffer):
    return lax.all_to_all(buffer, BOTH, 0, 0, tiled=True)


def grouped(buffer):
    return buffer.reshape((SLABS, 2) + buffer.shape[1:])


def flat(buffer):
    return buffer.reshape((128,) + buffer.shape[2:])


def body(field, cotangent, spectral_weight, point_weight, point_bias):
    ty, tyt, zb, tx, txi = (jnp.asarray(t) for t in tables())
    which = lax.axis_index("batch").astype(jnp.int32).reshape(1)
    zf = pltpu.VMEM((2048, 256), BF16)
    planes = pltpu.VMEM((512, 2048), BF16)
    wide = pltpu.VMEM((2048, 128), F32)
    gather = pltpu.VMEM((512, 512), BF16)
    held = pltpu.VMEM(PLANES, BF16)
    stage = pltpu.VMEM(BUFFER, BF16)
    sems = pltpu.SemaphoreType.DMA((X,))
    big = 8 * MIB
    swap = [(0, 1), (1, 0)]

    sent = call(
        field_kernel, struct(BUFFER, BF16), [HBM, HBM, HBM], HBM,
        [zf, planes, wide, held, pltpu.VMEM((64, NY), BF16), pltpu.VMEM((256, 512), BF16), stage,
         sems, pltpu.SemaphoreType.DMA, pltpu.SemaphoreType.DMA, sems], 2 * 10**9, big, 60, "field_planes",
    )(field, ty, zb)
    got = exchange(sent)
    pre = call(
        pre_kernel, struct(PLANES, BF16), [HBM, VMEM, VMEM], HBM,
        [held, held, sems, sems], 2 * 10**9, 2 * big, LIMIT, "point_map",
    )(field, point_weight, point_bias.reshape(1, C))
    got, pre = lax.optimization_barrier((got, pre))
    back, modes_u = call(
        mix_kernel,
        (struct((SLABS, 2, 16, 128), BF16), struct((512, 128), F32)),
        [SMEM] + [VMEM] * 4, (VMEM, VMEM),
        [pltpu.VMEM((32, 512), F32)],
        10**9, 3 * MIB, 32, "mix_modes",
    )(which, grouped(got), spectral_weight, tx, txi)
    got = exchange(flat(back))
    dpre, sent, bias_rows = call(
        signal_kernel,
        (struct(PLANES, BF16), struct(BUFFER, BF16), struct((8, 256), F32)),
        [VMEM, HBM, HBM, VMEM, VMEM, VMEM], (HBM, HBM, VMEM),
        [zf, planes, wide, gather, planes, held, held, stage, sems, sems, sems, sems],
        6 * 10**9, 3 * big, LIMIT, "signal",
    )(got, pre, cotangent, ty, tyt, zb)
    got = exchange(sent)
    extra, short_u = call(
        point_kernel, (struct((8, 128), F32), struct((128, 128), BF16)),
        [HBM, HBM, VMEM, VMEM], (VMEM, VMEM),
        [pltpu.VMEM((256, 256), F32), held, held, sems, sems],
        2 * 10**9, 2 * big, LIMIT, "point_gradient",
    )(field, dpre, bias_rows, modes_u)
    back, rows_d, short_d = call(
        adjoint_kernel,
        (struct((SLABS, 2, 24, 128), BF16), struct((32, 512), F32), struct((32, 512), BF16)),
        [SMEM] + [VMEM] * 5, (HBM, VMEM, VMEM),
        [pltpu.VMEM((512, 128), F32), pltpu.VMEM((512, 128), F32),
         pltpu.VMEM((SLABS, 2, 24, 128), BF16), sems],
        10**9, 3 * MIB, 32, "adjoint_modes",
    )(which, grouped(got), spectral_weight, tx, txi, extra)
    dpre, short_d, short_u = lax.optimization_barrier((dpre, short_d, short_u))
    got = exchange(flat(back))
    other_u = lax.ppermute(short_u, "batch", swap)
    other_d = lax.ppermute(short_d, "batch", swap)
    mapped = call(
        back_kernel, struct(PLANES, BF16), [HBM, VMEM], HBM,
        [held, held, sems, sems], 2 * 10**9, 2 * big, LIMIT, "point_map_back",
    )(dpre, point_weight)
    grad_spec = call(
        spec_kernel, struct((16, 2, C, 512), F32), [SMEM] + [VMEM] * 4, VMEM,
        [pltpu.VMEM((512, 128), F32), pltpu.VMEM((32, 512), F32)],
        10**7, 2 * MIB, 32, "spectral_gradient",
    )(which, modes_u, other_u, rows_d, other_d)
    input_grad, grad_point, grad_bias = call(
        final_kernel, (struct(GIVEN, BF16), struct((C, C), F32), struct((1, C), F32)),
        [VMEM, HBM, VMEM, VMEM], (HBM, VMEM, VMEM),
        [zf, pltpu.VMEM((3072, 128), F32), gather, planes, held, held, sems, sems],
        4 * 10**9, 2 * big, LIMIT, "input_gradient",
    )(got, mapped, tyt, zb)
    return input_grad, grad_spec, grad_point, grad_bias.reshape(C)


def solution(mesh):
    planes = P("batch", None, "slab", None, None)
    return jax.shard_map(
        body,
        mesh=mesh,
        in_specs=(planes, planes, P("slab", None, None, None), P(), P()),
        out_specs=(planes, P("slab", None, None, None), P(), P()),
        check_vma=False,
    )
```

```python
import math

import jax
import jax.numpy as jnp
import numpy as np
from jax import lax
from jax.experimental import pallas as pl
from jax.experimental.pallas import tpu as pltpu
from jax.sharding import PartitionSpec as P

C = 16
X = 8
NY = 256
NZ = 128
NX = 512
MODES = 32
SLABS = 64
CELLS = NX * NY * NZ
SCALE_F = 1.0 / math.sqrt(CELLS)
SCALE_I = 1.0 / math.sqrt(MODES**3)
SCALE_P = 1.0 / math.sqrt(2 * CELLS)
SCALE_W = math.sqrt(MODES**3 / (2 * CELLS))
GELU_A = math.sqrt(2.0 / math.pi)
GK = (GELU_A * 0.044715) ** (1.0 / 3.0)
GA = GELU_A / GK
BOTH = ("slab", "batch")
F32 = jnp.float32
BF16 = jnp.bfloat16
MIB = 1 << 20
LIMIT = 48
CUT = 8
AHEAD = 4
Z_CUTS = (4, 8)
HOLD = 3
PARTS = 8


def freqs(number, length):
    index = np.arange(number)
    return np.where(index < number // 2, index, index + length - number)


def angles(length, frequencies):
    product = (np.arange(length)[:, None] * frequencies[None, :]) % length
    return product * (2.0 * math.pi / length)


def tables():
    thy = angles(NY, freqs(MODES, NY))
    thz = angles(NZ, np.arange(MODES))
    thx = angles(NX, freqs(MODES, NX))
    ty = np.concatenate([np.cos(thy).T, -np.sin(thy).T], axis=0)
    cos, sin = np.cos(thz), np.sin(thz)
    rot = np.zeros((2, NZ, 2, MODES))
    rot[0, :, 0], rot[1, :, 0] = cos, sin
    rot[1, :, 1], rot[0, :, 1] = cos, -sin
    zb = rot.reshape(2, NZ, 2, 2, 2, 8).transpose(0, 1, 3, 2, 4, 5)
    zb = np.stack([zb, zb[:, :, :, :, ::-1]], axis=2)[:, :, :, :, :, :, None, :]
    zb = np.broadcast_to(zb, (2, NZ, 2, 2, 2, 2, 4, 8)).reshape(2 * NZ, 512)
    cs = np.stack([np.cos(thx), np.sin(thx)]).reshape(2, SLABS, X, MODES)
    tx = np.zeros((2, 2, 4, MODES, SLABS, 2, X))
    txi = np.zeros((SLABS, 2, X, 2, 2, MODES))
    for half in range(2):
        tx[half, :, :, :, :, half] = cs.transpose(0, 3, 1, 2)[:, None]
        txi[:, half, :, half] = cs.transpose(1, 2, 0, 3)
    return tuple(
        np.asarray(t, np.float32).astype(BF16)
        for t in (ty, ty.T, zb, tx.reshape(512, 1024), txi.reshape(1024, 128))
    )


def dot(left, right):
    return jnp.dot(left, right, preferred_element_type=F32)


def dot_nt(left, right):
    return lax.dot_general(left, right, (((1,), (1,)), ((), ())), preferred_element_type=F32)


def send_part(stage_ref, out_hbm, sem, i):
    count = out_hbm.shape[0] // PARTS
    part = pl.ds(i * count, count)
    return pltpu.make_async_copy(stage_ref.at[part], out_hbm.at[part], sem.at[i])


def finish(stage_ref, out_hbm, sem):
    for i in range(PARTS):
        send_part(stage_ref, out_hbm, sem, i).wait()


def build_z(zb_ref, zf_ref):
    channel = (lax.broadcasted_iota(jnp.int32, (2 * NZ, 256), 1) // 8) % 4
    for group in range(2):
        table = zb_ref[:, group * 256 : (group + 1) * 256].astype(F32)
        for c in range(4):
            row = group * 1024 + c * 256
            zf_ref[row : row + 256, :] = jnp.where(channel == c, table, 0.0).astype(BF16)


def low_lanes(rows):
    return lax.broadcasted_iota(jnp.int32, (rows, 128), 1) % 64 < 32


def z_part(planes_ref, zf_ref, wide_ref, start, count):
    low = low_lanes(count * 32)
    for half in range(2):
        row = half * 256 + start * 32
        first, second = (
            dot(
                planes_ref[row : row + count * 32, group * 1024 : (group + 1) * 1024],
                zf_ref[group * 1024 : (group + 1) * 1024, :],
            )
            for group in range(2)
        )
        for t in range(2):
            one, two = first[:, t * 128 : (t + 1) * 128], second[:, t * 128 : (t + 1) * 128]
            for j, value in enumerate((jnp.where(low, one, two), jnp.where(low, two, one))):
                for x in range(count):
                    place = (2 * t + j) * 16 + half * 8 + start + x
                    wide_ref[pl.ds(place, 32, stride=64), :] = value[x * 32 : (x + 1) * 32]


def z_send(wide_ref, stage_ref, out_hbm, sem):
    rows = 128 // PARTS
    for i in range(PARTS):
        stage_ref[i * rows : (i + 1) * rows] = (
            wide_ref[i * rows * 16 : (i + 1) * rows * 16, :].astype(BF16).reshape(rows, 16, 128)
        )
        send_part(stage_ref, out_hbm, sem, i).start()


def z_inverse(in_ref, zf_ref, wide_ref, gather_ref, rolled_ref):
    rows = in_ref.shape[1]
    wide_ref[...] = in_ref[...].astype(F32).reshape(128 * rows, 128)
    low = low_lanes(32)
    for half in range(2):
        for x in range(X):
            row = (half * 8 + x) * 32
            for t in range(2):
                even, odd = (
                    wide_ref[pl.ds((2 * t + j) * rows + half * 8 + x, 32, stride=4 * rows), :]
                    for j in range(2)
                )
                for group, value in enumerate((jnp.where(low, even, odd), jnp.where(low, odd, even))):
                    column = group * 256 + t * 128
                    gather_ref[row : row + 32, column : column + 128] = value.astype(BF16)
    for c in range(8):
        group = c // 4
        rolled_ref[:, c * 256 : (c + 1) * 256] = dot_nt(
            gather_ref[:, group * 256 : (group + 1) * 256], zf_ref[c * 256 : (c + 1) * 256, :]
        ).astype(BF16)


def y_forward(ty_ref, pair, planes_ref, x, op):
    result = dot(ty_ref[...], pair)
    half, first = op // 4, (op % 4) * 2
    row = half * 256 + x * 32
    rows = pl.ds(row if isinstance(x, int) else pl.multiple_of(row, 32), 32)
    for j in range(2):
        for part in range(2):
            column = (first + j) * 256 + part * 128
            planes_ref[rows, column : column + 128] = result[
                part * 32 : (part + 1) * 32, j * 128 : (j + 1) * 128
            ].astype(BF16)
    return result


def y_inverse(tyt_ref, rolled_ref, x, op):
    half, first = op // 4, (op % 4) * 2
    rows = pl.ds(pl.multiple_of(half * 256 + x * 32, 32), 32)
    blocks = []
    for j in range(2):
        column = (first + j) * 256
        blocks.append(
            jnp.concatenate(
                [
                    rolled_ref[rows, column : column + 128],
                    rolled_ref[rows, column + 128 : column + 256],
                ],
                axis=0,
            )
        )
    return dot(tyt_ref[...], jnp.concatenate(blocks, axis=1))


class Planes:
    def __init__(self, hbm_ref, vmem_ref, sem, given, out=False):
        self.hbm_ref, self.vmem_ref, self.sem, self.given, self.out = hbm_ref, vmem_ref, sem, given, out

    def copy(self, x, channels):
        far = self.hbm_ref.at[0, channels, x] if self.given else self.hbm_ref.at[x, channels]
        near = self.vmem_ref.at[x, channels]
        source, target = (near, far) if self.out else (far, near)
        return pltpu.make_async_copy(source, target, self.sem.at[x])

    def start(self, x):
        for c in range(0, C, CUT):
            self.copy(x, pl.ds(c, CUT)).start()

    def start_held(self, x, held):
        @pl.when(x == held - 1)
        def _():
            for first in range(held):
                self.start(first)

        @pl.when(x >= held)
        def _():
            self.start(x)

    def wait(self, x):
        self.copy(x, pl.ds(0, C)).wait()


def field_kernel(
    field_hbm, ty_hbm, zb_hbm, out_hbm,
    zf_ref, planes_ref, wide_ref, field_ref, ty_ref, zb_ref, stage_ref, sem, ty_sem, zb_sem, sent_sem,
):
    load = Planes(field_hbm, field_ref, sem, True)
    load_ty = pltpu.make_async_copy(ty_hbm, ty_ref, ty_sem)
    load_zb = pltpu.make_async_copy(zb_hbm, zb_ref, zb_sem)
    load_ty.start()
    load.start(0)
    load_zb.start()
    for x in range(1, AHEAD):
        load.start(x)
    load_ty.wait()
    load_zb.wait()
    build_z(zb_ref, zf_ref)
    for x in range(X):
        if x + AHEAD < X:
            load.start(x + AHEAD)
        load.wait(x)
        for op in range(8):
            pair = jnp.concatenate([field_ref[x, 2 * op], field_ref[x, 2 * op + 1]], axis=1)
            y_forward(ty_ref, pair, planes_ref, x, op)
        if x + 1 in Z_CUTS:
            start = max([0] + [cut for cut in Z_CUTS if cut < x + 1])
            z_part(planes_ref, zf_ref, wide_ref, start, x + 1 - start)
    z_send(wide_ref, stage_ref, out_hbm, sent_sem)
    finish(stage_ref, out_hbm, sent_sem)


def y_blocks(ref, x):
    return jnp.concatenate(
        [ref[x, :, b * 16 : (b + 1) * 16, :].reshape(256, 128) for b in range(16)], axis=1
    )


def owner_rows():
    group = lax.broadcasted_iota(jnp.int32, (256, 16), 0) // 16
    return jnp.where(group == lax.broadcasted_iota(jnp.int32, (256, 16), 1), 1.0, 0.0)


def same_row(value):
    row = lax.broadcasted_iota(jnp.int32, (256, 256), 0) % 16
    column = lax.broadcasted_iota(jnp.int32, (256, 256), 1) % 16
    return jnp.where(row == column, value, 0.0)


def map_planes(scale, in_hbm, map_rows, bias, out_hbm, in_ref, out_ref, in_sem, out_sem):
    load = Planes(in_hbm, in_ref, in_sem, len(in_hbm.shape) == 5)
    store = Planes(out_hbm, out_ref, out_sem, False, True)
    for x in range(X):
        load.start(x)
    kron = same_row(dot_nt(map_rows.astype(BF16), owner_rows().astype(BF16))).astype(BF16)

    def step(x, _):
        load.wait(x)
        for b in range(8):
            pair = jnp.concatenate(
                [in_ref[x, :, y : y + 16, :].reshape(256, 128) for y in (b * 32, b * 32 + 16)],
                axis=1,
            )
            result = dot(kron, pair)
            if bias is not None:
                result = result + bias
            result = (result * scale).astype(BF16)
            for j in range(2):
                y = b * 32 + j * 16
                out_ref[x, :, y : y + 16, :] = result[:, j * 128 : (j + 1) * 128].reshape(C, 16, 128)
        store.start(x)
        return 0

    lax.fori_loop(0, X, step, 0)
    for x in range(X):
        store.wait(x)


def pre_kernel(in_hbm, weight_ref, bias_ref, out_hbm, in_ref, out_ref, in_sem, out_sem):
    map_rows = dot_nt(owner_rows().astype(BF16), weight_ref[...])
    bias = jnp.sum(owner_rows() * bias_ref[...], axis=1, keepdims=True)
    map_planes(GK, in_hbm, map_rows, bias, out_hbm, in_ref, out_ref, in_sem, out_sem)


def back_kernel(in_hbm, weight_ref, out_hbm, in_ref, out_ref, in_sem, out_sem):
    map_rows = dot(owner_rows().astype(BF16), weight_ref[...])
    map_planes(0.5, in_hbm, map_rows, None, out_hbm, in_ref, out_ref, in_sem, out_sem)


def slope_of(h):
    one, add = BF16(1.0), BF16(GA)
    square = h * h
    t = jnp.tanh(h * (square + add))
    slope = h * (square * BF16(3.0) + add)
    return (one + t) * (one + (one - t) * slope)


def signal_kernel(
    in_ref, pre_hbm, cot_hbm, ty_ref, tyt_ref, zb_ref,
    dpre_hbm, out_hbm, bias_ref,
    zf_ref, planes_ref, wide_ref, gather_ref, rolled_ref, pre_ref, cot_ref, stage_ref,
    pre_sem, cot_sem, out_sem, sent_sem,
):
    load_pre = Planes(pre_hbm, pre_ref, pre_sem, False)
    load_cot = Planes(cot_hbm, cot_ref, cot_sem, True)
    store = Planes(dpre_hbm, cot_ref, out_sem, False, True)
    for x in range(X):
        load_pre.start(x)
        load_cot.start(x)
    build_z(zb_ref, zf_ref)
    z_inverse(in_ref, zf_ref, wide_ref, gather_ref, rolled_ref)
    bias_ref[...] = jnp.zeros_like(bias_ref)

    def step(x, _):
        load_pre.wait(x)
        load_cot.wait(x)
        for op in range(8):
            back = y_inverse(tyt_ref, rolled_ref, x, op)
            for j in range(2):
                o = 2 * op + j
                h = back[:, j * 128 : (j + 1) * 128].astype(BF16) + pre_ref[x, o]
                cot_ref[x, o] = slope_of(h) * cot_ref[x, o]
        store.start(x)
        for op in range(8):
            pair = jnp.concatenate([cot_ref[x, 2 * op], cot_ref[x, 2 * op + 1]], axis=1)
            result = y_forward(ty_ref, pair, planes_ref, x, op)
            bias_ref[op : op + 1, :] += result[0:1, :]
        return 0

    lax.fori_loop(0, X, step, 0)
    z_part(planes_ref, zf_ref, wide_ref, 0, X)
    z_send(wide_ref, stage_ref, out_hbm, sent_sem)
    for x in range(X):
        store.wait(x)
    finish(stage_ref, out_hbm, sent_sem)


def final_kernel(
    in_ref, mapped_hbm, tyt_ref, zb_ref, out_hbm, point_ref, bias_ref,
    zf_ref, wide_ref, gather_ref, rolled_ref, mapped_ref, out_ref, in_sem, out_sem,
):
    load = Planes(mapped_hbm, mapped_ref, in_sem, False)
    store = Planes(out_hbm, out_ref, out_sem, True, True)
    for x in range(X):
        load.start(x)
    build_z(zb_ref, zf_ref)
    z_inverse(in_ref, zf_ref, wide_ref, gather_ref, rolled_ref)

    def step(x, _):
        load.wait(x)
        for op in range(8):
            back = y_inverse(tyt_ref, rolled_ref, x, op)
            for j in range(2):
                o = 2 * op + j
                mapped = mapped_ref[x, o].astype(F32)
                out_ref[x, o] = (back[:, j * 128 : (j + 1) * 128] + mapped).astype(BF16)
        store.start_held(x, HOLD)
        return 0

    lax.fori_loop(0, X, step, 0)
    total = jnp.sum(wide_ref[...].reshape(128, 24, 128)[:, 16:24, :], axis=0) * (0.5 * SCALE_P)
    lane = lax.broadcasted_iota(jnp.int32, (16, 128), 1)
    row = lax.broadcasted_iota(jnp.int32, (16, 128), 0)
    point = jnp.where(row < 8, total[0:1] + total[2:3], total[1:2] + total[3:4])
    point = jnp.where(lane // 16 == row % 8, point, 0.0)
    bias = jnp.where(lane < 32, total[4:5], 0.0)
    fold = lax.broadcasted_iota(jnp.int32, (128, 16), 0) % 16
    fold = jnp.where(fold == lax.broadcasted_iota(jnp.int32, (128, 16), 1), 1.0, 0.0)
    exact = lax.Precision.HIGHEST
    point_ref[...] = jnp.dot(point, fold, preferred_element_type=F32, precision=exact)
    bias_ref[...] = jnp.dot(bias, fold, preferred_element_type=F32, precision=exact)[0:1]
    for x in range(X):
        store.wait(x)


def swapped(which, w):
    return which + w * (1 - 2 * which)


def x_forward(which, in_ref, tx_ref, scale, modes_ref):
    data = jnp.concatenate([in_ref[:, b].reshape(1024, 128) for b in range(2)], axis=1)
    raw = dot(tx_ref[...], data)
    lane = lax.broadcasted_iota(jnp.int32, (128, 128), 1)
    sign = jnp.where(lane < 64, scale, -scale)
    for half in range(2):
        for b in range(2):
            cosine = raw[half * 256 : half * 256 + 128, b * 128 : (b + 1) * 128]
            sine = raw[half * 256 + 128 : half * 256 + 256, b * 128 : (b + 1) * 128]
            modes = cosine * scale + pltpu.roll(sine, 64, 1) * sign
            turned = modes.T
            for s in range(2):
                for w in range(2):
                    row = (half * 2 + b) * 128 + s * 64 + swapped(which, w) * 32
                    place = s * 64 + w * 32
                    modes_ref[pl.ds(pl.multiple_of(row, 32), 32), :] = turned[place : place + 32]


def x_inverse(mixed, txi_ref, stage_ref, extra, send):
    lane = lax.broadcasted_iota(jnp.int32, (32, 128), 1)
    rows = []
    for half in range(2):
        turned = [mixed(half, b).T[:32] for b in range(2)]
        rows.append(jnp.concatenate(turned, axis=1))
        rows.append(
            jnp.concatenate(
                [jnp.where(lane < 64, -1.0, 1.0) * pltpu.roll(g, 64, 1) for g in turned], axis=1
            )
        )
    right = jnp.concatenate(rows, axis=0).astype(BF16)
    parts = 1 if send is None else PARTS
    count = SLABS // parts
    for i in range(parts):
        result = dot(txi_ref[i * count * 16 : (i + 1) * count * 16, :], right)
        if extra is None:
            result = result.astype(BF16)
        for b in range(2):
            block = result[:, b * 128 : (b + 1) * 128].reshape(count, 16, 128)
            if extra is not None:
                more = jnp.broadcast_to(extra[None], (count, 8, 128))
                block = jnp.concatenate([block, more], axis=1).astype(BF16)
            stage_ref[i * count : (i + 1) * count, b] = block
        if send is not None:
            send_part(stage_ref, *send, i).start()


def mix_kernel(which_ref, in_ref, weight_ref, tx_ref, txi_ref, out_ref, modes_ref, mixed_ref):
    which = which_ref[0]
    x_forward(which, in_ref, tx_ref, SCALE_F, modes_ref)
    first = which * 8
    for p in range(8):
        real = weight_ref[first + p, 0].astype(F32)
        imag = weight_ref[first + p, 1].astype(F32)
        for b in range(2):
            u = [
                [modes_ref[pl.ds((half * 2 + b) * 128 + s * 64 + p, 8, stride=8), :] for s in range(2)]
                for half in range(2)
            ]
            for q in range(4):
                total = [0.0, 0.0]
                for half in range(2):
                    w0 = real[half * 8 : half * 8 + 8, q * 128 : (q + 1) * 128]
                    w1 = imag[half * 8 : half * 8 + 8, q * 128 : (q + 1) * 128]
                    u0, u1 = u[half]
                    total[0] = total[0] + (u0 * w0 - u1 * w1)
                    total[1] = total[1] + (u0 * w1 + u1 * w0)
                for s in range(2):
                    row = (b * 2 + s) * 8 + p
                    mixed_ref[row : row + 1, q * 128 : (q + 1) * 128] = jnp.sum(
                        total[s], axis=0, keepdims=True
                    ) * (SCALE_I * GK)

    def mixed(half, b):
        pieces = []
        for s in range(2):
            row = (b * 2 + s) * 8
            for w in range(2):
                column = pl.multiple_of((half * 2 + swapped(which, w)) * 128, 128)
                piece = mixed_ref[row : row + 8, pl.ds(column, 128)]
                for r in range(4):
                    pieces.append(pltpu.roll(piece, 128 - 32 * r, 1) if r else piece)
        return jnp.concatenate(pieces, axis=0)

    x_inverse(mixed, txi_ref, out_ref, None, None)


def adjoint_kernel(
    which_ref, in_ref, weight_ref, tx_ref, txi_ref, extra_ref,
    out_hbm, rows_ref, short_ref, modes_ref, mixed_ref, stage_ref, sent_sem,
):
    which = which_ref[0]
    x_forward(which, in_ref, tx_ref, 0.5 * SCALE_I, modes_ref)
    group = lax.broadcasted_iota(jnp.int32, (8, 128), 1) // 32
    for b in range(2):
        for s in range(2):
            for q in range(4):
                half, c = q // 2, (q % 2) * 4
                row = (half * 2 + b) * 128 + s * 64 + c * 8
                value = modes_ref[row : row + 8, :]
                for r in range(1, 4):
                    value = jnp.where(group == r, modes_ref[row + 8 * r : row + 8 * r + 8, :], value)
                row = (b * 2 + s) * 8
                rows_ref[row : row + 8, q * 128 : (q + 1) * 128] = value
    first = which * 8
    for p in range(8):
        real = weight_ref[first + p, 0].astype(F32)
        imag = weight_ref[first + p, 1].astype(F32)
        for b in range(2):
            d0 = rows_ref[b * 16 + p : b * 16 + p + 1, :]
            d1 = rows_ref[b * 16 + 8 + p : b * 16 + 8 + p + 1, :]
            total0 = real * d0 + imag * d1
            total1 = real * d1 - imag * d0
            for s, total in enumerate((total0, total1)):
                folded = sum(total[:, q * 128 : (q + 1) * 128] for q in range(4))
                folded = folded + pltpu.roll(folded, 64, 1)
                folded = folded + pltpu.roll(folded, 32, 1)
                for half in range(2):
                    mixed_ref[pl.ds((half * 2 + b) * 128 + s * 64 + p, 8, stride=8), :] = (
                        folded[half * 8 : half * 8 + 8] * SCALE_F
                    )

    def mixed(half, b):
        pieces = []
        for s in range(2):
            for w in range(2):
                row = (half * 2 + b) * 128 + s * 64 + swapped(which, w) * 32
                pieces.append(mixed_ref[pl.ds(pl.multiple_of(row, 32), 32), :])
        return jnp.concatenate(pieces, axis=0)

    x_inverse(mixed, txi_ref, stage_ref, extra_ref[...], (out_hbm, sent_sem))
    short_ref[...] = rows_ref[...].astype(BF16)
    finish(stage_ref, out_hbm, sent_sem)


def spec_kernel(which_ref, u_ref, v_bf_ref, d_ref, e_bf_ref, out_ref, v_ref, e_ref):
    group = lax.broadcasted_iota(jnp.int32, (128, 128), 1) // 32
    short = v_bf_ref[...].astype(F32)
    for i in range(4):
        part = jnp.where(group == i, short, 0.0)
        part = part + pltpu.roll(part, 32, 1)
        v_ref[i * 128 : (i + 1) * 128, :] = part + pltpu.roll(part, 64, 1)
    e_ref[...] = e_bf_ref[...].astype(F32)
    mine = which_ref[0] * 8
    other = 8 - mine
    for start, modes_ref, rows_ref in ((mine, u_ref, d_ref), (other, v_ref, e_ref)):
        for p in range(8):
            for half in range(2):
                u = [
                    [
                        modes_ref[pl.ds((half * 2 + b) * 128 + s * 64 + p, 8, stride=8), :] * SCALE_W
                        for s in range(2)
                    ]
                    for b in range(2)
                ]
                for q in range(4):
                    real = imag = 0.0
                    for b in range(2):
                        d0 = rows_ref[b * 16 + p : b * 16 + p + 1, q * 128 : (q + 1) * 128]
                        d1 = rows_ref[b * 16 + 8 + p : b * 16 + 9 + p, q * 128 : (q + 1) * 128]
                        real = real + (u[b][0] * d0 + u[b][1] * d1)
                        imag = imag + (u[b][0] * d1 - u[b][1] * d0)
                    lanes = slice(q * 128, (q + 1) * 128)
                    out_ref[start + p, 0, half * 8 : half * 8 + 8, lanes] = real
                    out_ref[start + p, 1, half * 8 : half * 8 + 8, lanes] = imag


def point_kernel(
    field_hbm, dpre_hbm, bias_ref, modes_ref, out_ref, short_ref,
    acc_ref, field_ref, dpre_ref, field_sem, dpre_sem,
):
    load_field = Planes(field_hbm, field_ref, field_sem, True)
    load_dpre = Planes(dpre_hbm, dpre_ref, dpre_sem, False)
    for x in range(X):
        load_field.start(x)
        load_dpre.start(x)
    group = lax.broadcasted_iota(jnp.int32, (128, 128), 1) // 32
    short = modes_ref[0:128, :]
    for i in range(1, 4):
        short = jnp.where(group == i, modes_ref[i * 128 : (i + 1) * 128, :], short)
    short_ref[...] = short.astype(BF16)
    acc_ref[...] = jnp.zeros_like(acc_ref)

    def step(x, _):
        load_field.wait(x)
        load_dpre.wait(x)
        acc_ref[...] += dot_nt(y_blocks(field_ref, x), y_blocks(dpre_ref, x))
        return 0

    lax.fori_loop(0, X, step, 0)
    kept = same_row(acc_ref[...])
    rows = jnp.concatenate(
        [jnp.sum(kept[i * 16 : (i + 1) * 16], axis=0, keepdims=True) for i in range(16)], axis=0
    )
    owner = lax.broadcasted_iota(jnp.int32, (256, 128), 0) // 16
    column = lax.broadcasted_iota(jnp.int32, (256, 128), 1) % 16
    point = jnp.dot(
        rows,
        jnp.where(owner == column, 1.0, 0.0),
        preferred_element_type=F32,
        precision=lax.Precision.HIGHEST,
    )
    lane = lax.broadcasted_iota(jnp.int32, (8, 128), 1)
    row = lax.broadcasted_iota(jnp.int32, (8, 128), 0)
    first, second = (
        jnp.sum(jnp.where(lane // 16 == row, point[h * 8 : h * 8 + 8], 0.0), axis=0, keepdims=True)
        for h in range(2)
    )
    even = jnp.sum(bias_ref[:, 0:128], axis=1, keepdims=True)
    odd = jnp.sum(bias_ref[:, 128:256], axis=1, keepdims=True)
    bias = jnp.where(lane == 2 * row, even, jnp.where(lane == 2 * row + 1, odd, 0.0))
    bias = jnp.sum(bias, axis=0, keepdims=True)
    value = jnp.where(
        (row == 0) | (row == 2), first, jnp.where((row == 1) | (row == 3), second, 0.0)
    )
    value = jnp.where(row == 4, bias, value)
    high = value.astype(BF16).astype(F32)
    low = value - high
    packed = jnp.where(row < 2, high, jnp.where(row < 4, low, 0.0))
    packed = jnp.where((row == 4) & (lane < 16), high, packed)
    out_ref[...] = jnp.where((row == 4) & (lane >= 16), pltpu.roll(low, 16, 1), packed)


SMEM = pl.BlockSpec(memory_space=pltpu.SMEM)
VMEM = pl.BlockSpec(memory_space=pltpu.VMEM)
HBM = pl.BlockSpec(memory_space=pltpu.HBM)
BUFFER = (128, 16, 128)
PLANES = (X, C, NY, NZ)
GIVEN = (1, C, X, NY, NZ)


def struct(shape, dtype):
    return jax.ShapeDtypeStruct(shape, dtype)


def call(kernel, out_shape, in_specs, out_specs, scratch, flops, moved, limit, name):
    return pl.pallas_call(
        kernel,
        out_shape=out_shape,
        in_specs=in_specs,
        out_specs=out_specs,
        scratch_shapes=scratch,
        compiler_params=pltpu.CompilerParams(vmem_limit_bytes=limit * MIB),
        cost_estimate=pl.CostEstimate(flops=flops, bytes_accessed=moved, transcendentals=0),
        name=name,
    )


def exchange(buffer):
    return lax.all_to_all(buffer, BOTH, 0, 0, tiled=True)


def grouped(buffer):
    return buffer.reshape((SLABS, 2) + buffer.shape[1:])


def flat(buffer):
    return buffer.reshape((128,) + buffer.shape[2:])


def body(field, cotangent, spectral_weight, point_weight, point_bias):
    ty, tyt, zb, tx, txi = (jnp.asarray(t) for t in tables())
    which = lax.axis_index("batch").astype(jnp.int32).reshape(1)
    zf = pltpu.VMEM((2048, 256), BF16)
    planes = pltpu.VMEM((512, 2048), BF16)
    wide = pltpu.VMEM((2048, 128), F32)
    gather = pltpu.VMEM((512, 512), BF16)
    held = pltpu.VMEM(PLANES, BF16)
    stage = pltpu.VMEM(BUFFER, BF16)
    sems = pltpu.SemaphoreType.DMA((X,))
    big = 8 * MIB
    swap = [(0, 1), (1, 0)]

    sent = call(
        field_kernel, struct(BUFFER, BF16), [HBM, HBM, HBM], HBM,
        [zf, planes, wide, held, pltpu.VMEM((64, NY), BF16), pltpu.VMEM((256, 512), BF16), stage,
         sems, pltpu.SemaphoreType.DMA, pltpu.SemaphoreType.DMA, sems], 2 * 10**9, big, 60, "field_planes",
    )(field, ty, zb)
    got = exchange(sent)
    pre = call(
        pre_kernel, struct(PLANES, BF16), [HBM, VMEM, VMEM], HBM,
        [held, held, sems, sems], 2 * 10**9, 2 * big, LIMIT, "point_map",
    )(field, point_weight, point_bias.reshape(1, C))
    got, pre = lax.optimization_barrier((got, pre))
    back, modes_u = call(
        mix_kernel,
        (struct((SLABS, 2, 16, 128), BF16), struct((512, 128), F32)),
        [SMEM] + [VMEM] * 4, (VMEM, VMEM),
        [pltpu.VMEM((32, 512), F32)],
        10**9, 3 * MIB, 32, "mix_modes",
    )(which, grouped(got), spectral_weight, tx, txi)
    got = exchange(flat(back))
    dpre, sent, bias_rows = call(
        signal_kernel,
        (struct(PLANES, BF16), struct(BUFFER, BF16), struct((8, 256), F32)),
        [VMEM, HBM, HBM, VMEM, VMEM, VMEM], (HBM, HBM, VMEM),
        [zf, planes, wide, gather, planes, held, held, stage, sems, sems, sems, sems],
        6 * 10**9, 3 * big, LIMIT, "signal",
    )(got, pre, cotangent, ty, tyt, zb)
    got = exchange(sent)
    extra, short_u = call(
        point_kernel, (struct((8, 128), F32), struct((128, 128), BF16)),
        [HBM, HBM, VMEM, VMEM], (VMEM, VMEM),
        [pltpu.VMEM((256, 256), F32), held, held, sems, sems],
        2 * 10**9, 2 * big, LIMIT, "point_gradient",
    )(field, dpre, bias_rows, modes_u)
    back, rows_d, short_d = call(
        adjoint_kernel,
        (struct((SLABS, 2, 24, 128), BF16), struct((32, 512), F32), struct((32, 512), BF16)),
        [SMEM] + [VMEM] * 5, (HBM, VMEM, VMEM),
        [pltpu.VMEM((512, 128), F32), pltpu.VMEM((512, 128), F32),
         pltpu.VMEM((SLABS, 2, 24, 128), BF16), sems],
        10**9, 3 * MIB, 32, "adjoint_modes",
    )(which, grouped(got), spectral_weight, tx, txi, extra)
    dpre, short_d, short_u = lax.optimization_barrier((dpre, short_d, short_u))
    got = exchange(flat(back))
    other_u = lax.ppermute(short_u, "batch", swap)
    other_d = lax.ppermute(short_d, "batch", swap)
    mapped = call(
        back_kernel, struct(PLANES, BF16), [HBM, VMEM], HBM,
        [held, held, sems, sems], 2 * 10**9, 2 * big, LIMIT, "point_map_back",
    )(dpre, point_weight)
    grad_spec = call(
        spec_kernel, struct((16, 2, C, 512), F32), [SMEM] + [VMEM] * 4, VMEM,
        [pltpu.VMEM((512, 128), F32), pltpu.VMEM((32, 512), F32)],
        10**7, 2 * MIB, 32, "spectral_gradient",
    )(which, modes_u, other_u, rows_d, other_d)
    input_grad, grad_point, grad_bias = call(
        final_kernel, (struct(GIVEN, BF16), struct((C, C), F32), struct((1, C), F32)),
        [VMEM, HBM, VMEM, VMEM], (HBM, VMEM, VMEM),
        [zf, pltpu.VMEM((3072, 128), F32), gather, planes, held, held, sems, sems],
        4 * 10**9, 2 * big, LIMIT, "input_gradient",
    )(got, mapped, tyt, zb)
    return input_grad, grad_spec, grad_point, grad_bias.reshape(C)


def solution(mesh):
    planes = P("batch", None, "slab", None, None)
    return jax.shard_map(
        body,
        mesh=mesh,
        in_specs=(planes, planes, P("slab", None, None, None), P(), P()),
        out_specs=(planes, P("slab", None, None, None), P(), P()),
        check_vma=False,
    )
```

```python
import math

import jax
import jax.numpy as jnp
import numpy as np
from jax import lax
from jax.experimental import pallas as pl
from jax.experimental.pallas import tpu as pltpu
from jax.sharding import PartitionSpec as P

C = 16
X = 8
NY = 256
NZ = 128
NX = 512
MODES = 32
SLABS = 64
CELLS = NX * NY * NZ
SCALE_F = 1.0 / math.sqrt(CELLS)
SCALE_I = 1.0 / math.sqrt(MODES**3)
SCALE_P = 1.0 / math.sqrt(2 * CELLS)
SCALE_W = math.sqrt(MODES**3 / (2 * CELLS))
GELU_A = math.sqrt(2.0 / math.pi)
GK = (GELU_A * 0.044715) ** (1.0 / 3.0)
GA = GELU_A / GK
BOTH = ("slab", "batch")
F32 = jnp.float32
BF16 = jnp.bfloat16
MIB = 1 << 20
LIMIT = 48
CUT = 8
AHEAD = 4
Z_CUTS = (4, 8)
HOLD = 3
PARTS = 8


def freqs(number, length):
    index = np.arange(number)
    return np.where(index < number // 2, index, index + length - number)


def angles(length, frequencies):
    product = (np.arange(length)[:, None] * frequencies[None, :]) % length
    return product * (2.0 * math.pi / length)


def tables():
    thy = angles(NY, freqs(MODES, NY))
    thz = angles(NZ, np.arange(MODES))
    thx = angles(NX, freqs(MODES, NX))
    ty = np.concatenate([np.cos(thy).T, -np.sin(thy).T], axis=0)
    cos, sin = np.cos(thz), np.sin(thz)
    rot = np.zeros((2, NZ, 2, MODES))
    rot[0, :, 0], rot[1, :, 0] = cos, sin
    rot[1, :, 1], rot[0, :, 1] = cos, -sin
    zb = rot.reshape(2, NZ, 2, 2, 2, 8).transpose(0, 1, 3, 2, 4, 5)
    zb = np.stack([zb, zb[:, :, :, :, ::-1]], axis=2)[:, :, :, :, :, :, None, :]
    zb = np.broadcast_to(zb, (2, NZ, 2, 2, 2, 2, 4, 8)).reshape(2 * NZ, 512)
    cs = np.stack([np.cos(thx), np.sin(thx)]).reshape(2, SLABS, X, MODES)
    tx = np.zeros((2, 2, 4, MODES, SLABS, 2, X))
    txi = np.zeros((SLABS, 2, X, 2, 2, MODES))
    for half in range(2):
        tx[half, :, :, :, :, half] = cs.transpose(0, 3, 1, 2)[:, None]
        txi[:, half, :, half] = cs.transpose(1, 2, 0, 3)
    return tuple(
        np.asarray(t, np.float32).astype(BF16)
        for t in (ty, ty.T, zb, tx.reshape(512, 1024), txi.reshape(1024, 128))
    )


def dot(left, right):
    return jnp.dot(left, right, preferred_element_type=F32)


def dot_nt(left, right):
    return lax.dot_general(left, right, (((1,), (1,)), ((), ())), preferred_element_type=F32)


def send_part(stage_ref, out_hbm, sem, i):
    count = out_hbm.shape[0] // PARTS
    part = pl.ds(i * count, count)
    return pltpu.make_async_copy(stage_ref.at[part], out_hbm.at[part], sem.at[i])


def finish(stage_ref, out_hbm, sem):
    for i in range(PARTS):
        send_part(stage_ref, out_hbm, sem, i).wait()


def build_z(zb_ref, zf_ref):
    channel = (lax.broadcasted_iota(jnp.int32, (2 * NZ, 256), 1) // 8) % 4
    for group in range(2):
        table = zb_ref[:, group * 256 : (group + 1) * 256].astype(F32)
        for c in range(4):
            row = group * 1024 + c * 256
            zf_ref[row : row + 256, :] = jnp.where(channel == c, table, 0.0).astype(BF16)


def low_lanes(rows):
    return lax.broadcasted_iota(jnp.int32, (rows, 128), 1) % 64 < 32


def z_part(planes_ref, zf_ref, wide_ref, start, count):
    low = low_lanes(count * 32)
    for half in range(2):
        row = half * 256 + start * 32
        first, second = (
            dot(
                planes_ref[row : row + count * 32, group * 1024 : (group + 1) * 1024],
                zf_ref[group * 1024 : (group + 1) * 1024, :],
            )
            for group in range(2)
        )
        for t in range(2):
            one, two = first[:, t * 128 : (t + 1) * 128], second[:, t * 128 : (t + 1) * 128]
            for j, value in enumerate((jnp.where(low, one, two), jnp.where(low, two, one))):
                for x in range(count):
                    place = (2 * t + j) * 16 + half * 8 + start + x
                    wide_ref[pl.ds(place, 32, stride=64), :] = value[x * 32 : (x + 1) * 32]


def z_send(wide_ref, stage_ref, out_hbm, sem):
    rows = 128 // PARTS
    for i in range(PARTS):
        stage_ref[i * rows : (i + 1) * rows] = (
            wide_ref[i * rows * 16 : (i + 1) * rows * 16, :].astype(BF16).reshape(rows, 16, 128)
        )
        send_part(stage_ref, out_hbm, sem, i).start()


def z_inverse(in_ref, zf_ref, wide_ref, gather_ref, rolled_ref):
    rows = in_ref.shape[1]
    wide_ref[0 : 128 * rows, :] = in_ref[...].astype(F32).reshape(128 * rows, 128)
    low = low_lanes(32)
    for half in range(2):
        for x in range(X):
            row = (half * 8 + x) * 32
            for t in range(2):
                even, odd = (
                    wide_ref[pl.ds((2 * t + j) * rows + half * 8 + x, 32, stride=4 * rows), :]
                    for j in range(2)
                )
                for group, value in enumerate((jnp.where(low, even, odd), jnp.where(low, odd, even))):
                    column = group * 256 + t * 128
                    gather_ref[row : row + 32, column : column + 128] = value.astype(BF16)
    for c in range(8):
        group = c // 4
        rolled_ref[:, c * 256 : (c + 1) * 256] = dot_nt(
            gather_ref[:, group * 256 : (group + 1) * 256], zf_ref[c * 256 : (c + 1) * 256, :]
        ).astype(BF16)


def y_forward(ty_ref, pair, planes_ref, x, op):
    result = dot(ty_ref[...], pair)
    half, first = op // 4, (op % 4) * 2
    row = half * 256 + x * 32
    rows = pl.ds(row if isinstance(x, int) else pl.multiple_of(row, 32), 32)
    for j in range(2):
        for part in range(2):
            column = (first + j) * 256 + part * 128
            planes_ref[rows, column : column + 128] = result[
                part * 32 : (part + 1) * 32, j * 128 : (j + 1) * 128
            ].astype(BF16)
    return result


def y_inverse(tyt_ref, rolled_ref, x, op):
    half, first = op // 4, (op % 4) * 2
    rows = pl.ds(pl.multiple_of(half * 256 + x * 32, 32), 32)
    blocks = []
    for j in range(2):
        column = (first + j) * 256
        blocks.append(
            jnp.concatenate(
                [
                    rolled_ref[rows, column : column + 128],
                    rolled_ref[rows, column + 128 : column + 256],
                ],
                axis=0,
            )
        )
    return dot(tyt_ref[...], jnp.concatenate(blocks, axis=1))


class Planes:
    def __init__(self, hbm_ref, vmem_ref, sem, given, out=False):
        self.hbm_ref, self.vmem_ref, self.sem, self.given, self.out = hbm_ref, vmem_ref, sem, given, out

    def copy(self, x, channels):
        far = self.hbm_ref.at[0, channels, x] if self.given else self.hbm_ref.at[x, channels]
        near = self.vmem_ref.at[x, channels]
        source, target = (near, far) if self.out else (far, near)
        return pltpu.make_async_copy(source, target, self.sem.at[x])

    def start(self, x):
        for c in range(0, C, CUT):
            self.copy(x, pl.ds(c, CUT)).start()

    def start_held(self, x, held):
        @pl.when(x == held - 1)
        def _():
            for first in range(held):
                self.start(first)

        @pl.when(x >= held)
        def _():
            self.start(x)

    def wait(self, x):
        self.copy(x, pl.ds(0, C)).wait()


def field_kernel(
    field_hbm, ty_hbm, zb_hbm, out_hbm,
    zf_ref, planes_ref, wide_ref, field_ref, ty_ref, zb_ref, stage_ref, sem, ty_sem, zb_sem, sent_sem,
):
    load = Planes(field_hbm, field_ref, sem, True)
    load_ty = pltpu.make_async_copy(ty_hbm, ty_ref, ty_sem)
    load_zb = pltpu.make_async_copy(zb_hbm, zb_ref, zb_sem)
    load_ty.start()
    load.start(0)
    load_zb.start()
    for x in range(1, AHEAD):
        load.start(x)
    load_ty.wait()
    load_zb.wait()
    build_z(zb_ref, zf_ref)
    for x in range(X):
        if x + AHEAD < X:
            load.start(x + AHEAD)
        load.wait(x)
        for op in range(8):
            pair = jnp.concatenate([field_ref[x, 2 * op], field_ref[x, 2 * op + 1]], axis=1)
            y_forward(ty_ref, pair, planes_ref, x, op)
        if x + 1 in Z_CUTS:
            start = max([0] + [cut for cut in Z_CUTS if cut < x + 1])
            z_part(planes_ref, zf_ref, wide_ref, start, x + 1 - start)
    z_send(wide_ref, stage_ref, out_hbm, sent_sem)
    finish(stage_ref, out_hbm, sent_sem)


def y_blocks(ref, x):
    return jnp.concatenate(
        [ref[x, :, b * 16 : (b + 1) * 16, :].reshape(256, 128) for b in range(16)], axis=1
    )


def owner_rows():
    group = lax.broadcasted_iota(jnp.int32, (256, 16), 0) // 16
    return jnp.where(group == lax.broadcasted_iota(jnp.int32, (256, 16), 1), 1.0, 0.0)


def same_row(value):
    row = lax.broadcasted_iota(jnp.int32, (256, 256), 0) % 16
    column = lax.broadcasted_iota(jnp.int32, (256, 256), 1) % 16
    return jnp.where(row == column, value, 0.0)


def map_planes(scale, in_hbm, map_rows, bias, out_hbm, in_ref, out_ref, in_sem, out_sem):
    load = Planes(in_hbm, in_ref, in_sem, len(in_hbm.shape) == 5)
    store = Planes(out_hbm, out_ref, out_sem, False, True)
    for x in range(X):
        load.start(x)
    kron = same_row(dot_nt(map_rows.astype(BF16), owner_rows().astype(BF16))).astype(BF16)

    def step(x, _):
        load.wait(x)
        for b in range(8):
            pair = jnp.concatenate(
                [in_ref[x, :, y : y + 16, :].reshape(256, 128) for y in (b * 32, b * 32 + 16)],
                axis=1,
            )
            result = dot(kron, pair)
            if bias is not None:
                result = result + bias
            result = (result * scale).astype(BF16)
            for j in range(2):
                y = b * 32 + j * 16
                out_ref[x, :, y : y + 16, :] = result[:, j * 128 : (j + 1) * 128].reshape(C, 16, 128)
        store.start(x)
        return 0

    lax.fori_loop(0, X, step, 0)
    for x in range(X):
        store.wait(x)


def pre_kernel(in_hbm, weight_ref, bias_ref, out_hbm, in_ref, out_ref, in_sem, out_sem):
    map_rows = dot_nt(owner_rows().astype(BF16), weight_ref[...])
    bias = jnp.sum(owner_rows() * bias_ref[...], axis=1, keepdims=True)
    map_planes(GK, in_hbm, map_rows, bias, out_hbm, in_ref, out_ref, in_sem, out_sem)


def back_kernel(in_hbm, weight_ref, out_hbm, in_ref, out_ref, in_sem, out_sem):
    map_rows = dot(owner_rows().astype(BF16), weight_ref[...])
    map_planes(0.5, in_hbm, map_rows, None, out_hbm, in_ref, out_ref, in_sem, out_sem)


def slope_of(h):
    one, add = BF16(1.0), BF16(GA)
    square = h * h
    t = jnp.tanh(h * (square + add))
    slope = h * (square * BF16(3.0) + add)
    return (one + t) * (one + (one - t) * slope)


def signal_kernel(
    in_ref, pre_hbm, cot_hbm, ty_ref, tyt_ref, zb_ref,
    dpre_hbm, out_hbm, bias_ref,
    zf_ref, planes_ref, wide_ref, gather_ref, rolled_ref, pre_ref, cot_ref, stage_ref,
    pre_sem, cot_sem, out_sem, sent_sem,
):
    load_pre = Planes(pre_hbm, pre_ref, pre_sem, False)
    load_cot = Planes(cot_hbm, cot_ref, cot_sem, True)
    store = Planes(dpre_hbm, cot_ref, out_sem, False, True)
    for x in range(X):
        load_pre.start(x)
        load_cot.start(x)
    build_z(zb_ref, zf_ref)
    z_inverse(in_ref, zf_ref, wide_ref, gather_ref, rolled_ref)
    bias_ref[...] = jnp.zeros_like(bias_ref)

    def step(x, _):
        load_pre.wait(x)
        load_cot.wait(x)
        for op in range(8):
            back = y_inverse(tyt_ref, rolled_ref, x, op)
            for j in range(2):
                o = 2 * op + j
                h = back[:, j * 128 : (j + 1) * 128].astype(BF16) + pre_ref[x, o]
                cot_ref[x, o] = slope_of(h) * cot_ref[x, o]
        store.start(x)
        for op in range(8):
            pair = jnp.concatenate([cot_ref[x, 2 * op], cot_ref[x, 2 * op + 1]], axis=1)
            result = y_forward(ty_ref, pair, planes_ref, x, op)
            bias_ref[op : op + 1, :] += result[0:1, :]
        return 0

    lax.fori_loop(0, X, step, 0)
    z_part(planes_ref, zf_ref, wide_ref, 0, X)
    z_send(wide_ref, stage_ref, out_hbm, sent_sem)
    for x in range(X):
        store.wait(x)
    finish(stage_ref, out_hbm, sent_sem)


def final_kernel(
    in_ref, mapped_hbm, tyt_ref, zb_ref, out_hbm, point_ref, bias_ref,
    zf_ref, wide_ref, gather_ref, rolled_ref, mapped_ref, out_ref, in_sem, out_sem,
):
    load = Planes(mapped_hbm, mapped_ref, in_sem, False)
    store = Planes(out_hbm, out_ref, out_sem, True, True)
    for x in range(X):
        load.start(x)
    build_z(zb_ref, zf_ref)
    z_inverse(in_ref, zf_ref, wide_ref, gather_ref, rolled_ref)

    def step(x, _):
        load.wait(x)
        for op in range(8):
            back = y_inverse(tyt_ref, rolled_ref, x, op)
            for j in range(2):
                o = 2 * op + j
                mapped = mapped_ref[x, o].astype(F32)
                out_ref[x, o] = (back[:, j * 128 : (j + 1) * 128] + mapped).astype(BF16)
        store.start_held(x, HOLD)
        return 0

    lax.fori_loop(0, X, step, 0)
    total = jnp.sum(wide_ref[0:3072, :].reshape(128, 24, 128)[:, 16:24, :], axis=0) * (0.5 * SCALE_P)
    lane = lax.broadcasted_iota(jnp.int32, (16, 128), 1)
    row = lax.broadcasted_iota(jnp.int32, (16, 128), 0)
    point = jnp.where(row < 8, total[0:1] + total[2:3], total[1:2] + total[3:4])
    point = jnp.where(lane // 16 == row % 8, point, 0.0)
    bias = jnp.where(lane < 32, total[4:5], 0.0)
    fold = lax.broadcasted_iota(jnp.int32, (128, 16), 0) % 16
    fold = jnp.where(fold == lax.broadcasted_iota(jnp.int32, (128, 16), 1), 1.0, 0.0)
    exact = lax.Precision.HIGHEST
    point_ref[...] = jnp.dot(point, fold, preferred_element_type=F32, precision=exact)
    bias_ref[...] = jnp.dot(bias, fold, preferred_element_type=F32, precision=exact)[0:1]
    for x in range(X):
        store.wait(x)


def swapped(which, w):
    return which + w * (1 - 2 * which)


def x_forward(which, in_ref, tx_ref, scale, modes_ref):
    data = jnp.concatenate([in_ref[:, b].reshape(1024, 128) for b in range(2)], axis=1)
    raw = dot(tx_ref[...], data)
    lane = lax.broadcasted_iota(jnp.int32, (128, 128), 1)
    sign = jnp.where(lane < 64, scale, -scale)
    for half in range(2):
        for b in range(2):
            cosine = raw[half * 256 : half * 256 + 128, b * 128 : (b + 1) * 128]
            sine = raw[half * 256 + 128 : half * 256 + 256, b * 128 : (b + 1) * 128]
            modes = cosine * scale + pltpu.roll(sine, 64, 1) * sign
            turned = modes.T
            for s in range(2):
                for w in range(2):
                    row = (half * 2 + b) * 128 + s * 64 + swapped(which, w) * 32
                    place = s * 64 + w * 32
                    modes_ref[pl.ds(pl.multiple_of(row, 32), 32), :] = turned[place : place + 32]


def x_inverse(mixed, txi_ref, stage_ref, extra, send):
    lane = lax.broadcasted_iota(jnp.int32, (32, 128), 1)
    rows = []
    for half in range(2):
        turned = [mixed(half, b).T[:32] for b in range(2)]
        rows.append(jnp.concatenate(turned, axis=1))
        rows.append(
            jnp.concatenate(
                [jnp.where(lane < 64, -1.0, 1.0) * pltpu.roll(g, 64, 1) for g in turned], axis=1
            )
        )
    right = jnp.concatenate(rows, axis=0).astype(BF16)
    parts = 1 if send is None else PARTS
    count = SLABS // parts
    for i in range(parts):
        result = dot(txi_ref[i * count * 16 : (i + 1) * count * 16, :], right)
        if extra is None:
            result = result.astype(BF16)
        for b in range(2):
            block = result[:, b * 128 : (b + 1) * 128].reshape(count, 16, 128)
            if extra is not None:
                more = jnp.broadcast_to(extra[None], (count, 8, 128))
                block = jnp.concatenate([block, more], axis=1).astype(BF16)
            stage_ref[i * count : (i + 1) * count, b] = block
        if send is not None:
            send_part(stage_ref, *send, i).start()


def mix_kernel(which_ref, in_ref, weight_ref, tx_ref, txi_ref, out_ref, modes_ref, mixed_ref):
    which = which_ref[0]
    x_forward(which, in_ref, tx_ref, SCALE_F, modes_ref)
    first = which * 8
    for p in range(8):
        real = weight_ref[first + p, 0].astype(F32)
        imag = weight_ref[first + p, 1].astype(F32)
        for b in range(2):
            u = [
                [modes_ref[pl.ds((half * 2 + b) * 128 + s * 64 + p, 8, stride=8), :] for s in range(2)]
                for half in range(2)
            ]
            for q in range(4):
                total = [0.0, 0.0]
                for half in range(2):
                    w0 = real[half * 8 : half * 8 + 8, q * 128 : (q + 1) * 128]
                    w1 = imag[half * 8 : half * 8 + 8, q * 128 : (q + 1) * 128]
                    u0, u1 = u[half]
                    total[0] = total[0] + (u0 * w0 - u1 * w1)
                    total[1] = total[1] + (u0 * w1 + u1 * w0)
                for s in range(2):
                    row = (b * 2 + s) * 8 + p
                    mixed_ref[row : row + 1, q * 128 : (q + 1) * 128] = jnp.sum(
                        total[s], axis=0, keepdims=True
                    ) * (SCALE_I * GK)

    def mixed(half, b):
        pieces = []
        for s in range(2):
            row = (b * 2 + s) * 8
            for w in range(2):
                column = pl.multiple_of((half * 2 + swapped(which, w)) * 128, 128)
                piece = mixed_ref[row : row + 8, pl.ds(column, 128)]
                for r in range(4):
                    pieces.append(pltpu.roll(piece, 128 - 32 * r, 1) if r else piece)
        return jnp.concatenate(pieces, axis=0)

    x_inverse(mixed, txi_ref, out_ref, None, None)


def adjoint_kernel(
    which_ref, in_ref, weight_ref, tx_ref, txi_ref, extra_ref,
    out_hbm, rows_ref, short_ref, modes_ref, mixed_ref, stage_ref, sent_sem,
):
    which = which_ref[0]
    x_forward(which, in_ref, tx_ref, 0.5 * SCALE_I, modes_ref)
    group = lax.broadcasted_iota(jnp.int32, (8, 128), 1) // 32
    for b in range(2):
        for s in range(2):
            for q in range(4):
                half, c = q // 2, (q % 2) * 4
                row = (half * 2 + b) * 128 + s * 64 + c * 8
                value = modes_ref[row : row + 8, :]
                for r in range(1, 4):
                    value = jnp.where(group == r, modes_ref[row + 8 * r : row + 8 * r + 8, :], value)
                row = (b * 2 + s) * 8
                rows_ref[row : row + 8, q * 128 : (q + 1) * 128] = value
    first = which * 8
    for p in range(8):
        real = weight_ref[first + p, 0].astype(F32)
        imag = weight_ref[first + p, 1].astype(F32)
        for b in range(2):
            d0 = rows_ref[b * 16 + p : b * 16 + p + 1, :]
            d1 = rows_ref[b * 16 + 8 + p : b * 16 + 8 + p + 1, :]
            total0 = real * d0 + imag * d1
            total1 = real * d1 - imag * d0
            for s, total in enumerate((total0, total1)):
                folded = sum(total[:, q * 128 : (q + 1) * 128] for q in range(4))
                folded = folded + pltpu.roll(folded, 64, 1)
                folded = folded + pltpu.roll(folded, 32, 1)
                for half in range(2):
                    mixed_ref[pl.ds((half * 2 + b) * 128 + s * 64 + p, 8, stride=8), :] = (
                        folded[half * 8 : half * 8 + 8] * SCALE_F
                    )

    def mixed(half, b):
        pieces = []
        for s in range(2):
            for w in range(2):
                row = (half * 2 + b) * 128 + s * 64 + swapped(which, w) * 32
                pieces.append(mixed_ref[pl.ds(pl.multiple_of(row, 32), 32), :])
        return jnp.concatenate(pieces, axis=0)

    x_inverse(mixed, txi_ref, stage_ref, extra_ref[...], (out_hbm, sent_sem))
    short_ref[...] = rows_ref[...].astype(BF16)
    finish(stage_ref, out_hbm, sent_sem)


def spec_kernel(which_ref, u_ref, v_bf_ref, d_ref, e_bf_ref, out_ref, v_ref, e_ref):
    group = lax.broadcasted_iota(jnp.int32, (128, 128), 1) // 32
    short = v_bf_ref[...].astype(F32)
    for i in range(4):
        part = jnp.where(group == i, short, 0.0)
        part = part + pltpu.roll(part, 32, 1)
        v_ref[i * 128 : (i + 1) * 128, :] = part + pltpu.roll(part, 64, 1)
    e_ref[...] = e_bf_ref[...].astype(F32)
    mine = which_ref[0] * 8
    other = 8 - mine
    for start, modes_ref, rows_ref in ((mine, u_ref, d_ref), (other, v_ref, e_ref)):
        for p in range(8):
            for half in range(2):
                u = [
                    [
                        modes_ref[pl.ds((half * 2 + b) * 128 + s * 64 + p, 8, stride=8), :] * SCALE_W
                        for s in range(2)
                    ]
                    for b in range(2)
                ]
                for q in range(4):
                    real = imag = 0.0
                    for b in range(2):
                        d0 = rows_ref[b * 16 + p : b * 16 + p + 1, q * 128 : (q + 1) * 128]
                        d1 = rows_ref[b * 16 + 8 + p : b * 16 + 9 + p, q * 128 : (q + 1) * 128]
                        real = real + (u[b][0] * d0 + u[b][1] * d1)
                        imag = imag + (u[b][0] * d1 - u[b][1] * d0)
                    lanes = slice(q * 128, (q + 1) * 128)
                    out_ref[start + p, 0, half * 8 : half * 8 + 8, lanes] = real
                    out_ref[start + p, 1, half * 8 : half * 8 + 8, lanes] = imag


def point_kernel(
    field_hbm, dpre_hbm, bias_ref, modes_ref, out_ref, short_ref,
    acc_ref, field_ref, dpre_ref, field_sem, dpre_sem,
):
    load_field = Planes(field_hbm, field_ref, field_sem, True)
    load_dpre = Planes(dpre_hbm, dpre_ref, dpre_sem, False)
    for x in range(X):
        load_field.start(x)
        load_dpre.start(x)
    group = lax.broadcasted_iota(jnp.int32, (128, 128), 1) // 32
    short = modes_ref[0:128, :]
    for i in range(1, 4):
        short = jnp.where(group == i, modes_ref[i * 128 : (i + 1) * 128, :], short)
    short_ref[...] = short.astype(BF16)
    acc_ref[...] = jnp.zeros_like(acc_ref)

    def step(x, _):
        load_field.wait(x)
        load_dpre.wait(x)
        acc_ref[...] += dot_nt(y_blocks(field_ref, x), y_blocks(dpre_ref, x))
        return 0

    lax.fori_loop(0, X, step, 0)
    kept = same_row(acc_ref[...])
    rows = jnp.concatenate(
        [jnp.sum(kept[i * 16 : (i + 1) * 16], axis=0, keepdims=True) for i in range(16)], axis=0
    )
    owner = lax.broadcasted_iota(jnp.int32, (256, 128), 0) // 16
    column = lax.broadcasted_iota(jnp.int32, (256, 128), 1) % 16
    point = jnp.dot(
        rows,
        jnp.where(owner == column, 1.0, 0.0),
        preferred_element_type=F32,
        precision=lax.Precision.HIGHEST,
    )
    lane = lax.broadcasted_iota(jnp.int32, (8, 128), 1)
    row = lax.broadcasted_iota(jnp.int32, (8, 128), 0)
    first, second = (
        jnp.sum(jnp.where(lane // 16 == row, point[h * 8 : h * 8 + 8], 0.0), axis=0, keepdims=True)
        for h in range(2)
    )
    even = jnp.sum(bias_ref[:, 0:128], axis=1, keepdims=True)
    odd = jnp.sum(bias_ref[:, 128:256], axis=1, keepdims=True)
    bias = jnp.where(lane == 2 * row, even, jnp.where(lane == 2 * row + 1, odd, 0.0))
    bias = jnp.sum(bias, axis=0, keepdims=True)
    value = jnp.where(
        (row == 0) | (row == 2), first, jnp.where((row == 1) | (row == 3), second, 0.0)
    )
    value = jnp.where(row == 4, bias, value)
    high = value.astype(BF16).astype(F32)
    low = value - high
    packed = jnp.where(row < 2, high, jnp.where(row < 4, low, 0.0))
    packed = jnp.where((row == 4) & (lane < 16), high, packed)
    out_ref[...] = jnp.where((row == 4) & (lane >= 16), pltpu.roll(low, 16, 1), packed)


SMEM = pl.BlockSpec(memory_space=pltpu.SMEM)
VMEM = pl.BlockSpec(memory_space=pltpu.VMEM)
HBM = pl.BlockSpec(memory_space=pltpu.HBM)
BUFFER = (128, 16, 128)
PLANES = (X, C, NY, NZ)
GIVEN = (1, C, X, NY, NZ)


def struct(shape, dtype):
    return jax.ShapeDtypeStruct(shape, dtype)


def call(kernel, out_shape, in_specs, out_specs, scratch, flops, moved, limit, name):
    return pl.pallas_call(
        kernel,
        out_shape=out_shape,
        in_specs=in_specs,
        out_specs=out_specs,
        scratch_shapes=scratch,
        compiler_params=pltpu.CompilerParams(vmem_limit_bytes=limit * MIB),
        cost_estimate=pl.CostEstimate(flops=flops, bytes_accessed=moved, transcendentals=0),
        name=name,
    )


def exchange(buffer):
    return lax.all_to_all(buffer, BOTH, 0, 0, tiled=True)


def grouped(buffer):
    return buffer.reshape((SLABS, 2) + buffer.shape[1:])


def flat(buffer):
    return buffer.reshape((128,) + buffer.shape[2:])


def body(field, cotangent, spectral_weight, point_weight, point_bias):
    ty, tyt, zb, tx, txi = (jnp.asarray(t) for t in tables())
    which = lax.axis_index("batch").astype(jnp.int32).reshape(1)
    zf = pltpu.VMEM((2048, 256), BF16)
    planes = pltpu.VMEM((512, 2048), BF16)
    wide = pltpu.VMEM((2048 + 64, 128), F32)
    gather = pltpu.VMEM((512, 512), BF16)
    held = pltpu.VMEM(PLANES, BF16)
    stage = pltpu.VMEM(BUFFER, BF16)
    sems = pltpu.SemaphoreType.DMA((X,))
    big = 8 * MIB
    swap = [(0, 1), (1, 0)]

    sent = call(
        field_kernel, struct(BUFFER, BF16), [HBM, HBM, HBM], HBM,
        [zf, planes, wide, held, pltpu.VMEM((64, NY), BF16), pltpu.VMEM((256, 512), BF16), stage,
         sems, pltpu.SemaphoreType.DMA, pltpu.SemaphoreType.DMA, sems], 2 * 10**9, big, 60, "field_planes",
    )(field, ty, zb)
    got = exchange(sent)
    pre = call(
        pre_kernel, struct(PLANES, BF16), [HBM, VMEM, VMEM], HBM,
        [held, held, sems, sems], 2 * 10**9, 2 * big, LIMIT, "point_map",
    )(field, point_weight, point_bias.reshape(1, C))
    got, pre = lax.optimization_barrier((got, pre))
    back, modes_u = call(
        mix_kernel,
        (struct((SLABS, 2, 16, 128), BF16), struct((520, 128), F32)),
        [SMEM] + [VMEM] * 4, (VMEM, VMEM),
        [pltpu.VMEM((32, 512), F32)],
        10**9, 3 * MIB, 32, "mix_modes",
    )(which, grouped(got), spectral_weight, tx, txi)
    got = exchange(flat(back))
    dpre, sent, bias_rows = call(
        signal_kernel,
        (struct(PLANES, BF16), struct(BUFFER, BF16), struct((8, 256), F32)),
        [VMEM, HBM, HBM, VMEM, VMEM, VMEM], (HBM, HBM, VMEM),
        [zf, planes, wide, gather, planes, held, held, stage, sems, sems, sems, sems],
        6 * 10**9, 3 * big, LIMIT, "signal",
    )(got, pre, cotangent, ty, tyt, zb)
    got = exchange(sent)
    extra, short_u = call(
        point_kernel, (struct((8, 128), F32), struct((128, 128), BF16)),
        [HBM, HBM, VMEM, VMEM], (VMEM, VMEM),
        [pltpu.VMEM((256, 256), F32), held, held, sems, sems],
        2 * 10**9, 2 * big, LIMIT, "point_gradient",
    )(field, dpre, bias_rows, modes_u)
    back, rows_d, short_d = call(
        adjoint_kernel,
        (struct((SLABS, 2, 24, 128), BF16), struct((32, 512), F32), struct((32, 512), BF16)),
        [SMEM] + [VMEM] * 5, (HBM, VMEM, VMEM),
        [pltpu.VMEM((520, 128), F32), pltpu.VMEM((520, 128), F32),
         pltpu.VMEM((SLABS, 2, 24, 128), BF16), sems],
        10**9, 3 * MIB, 32, "adjoint_modes",
    )(which, grouped(got), spectral_weight, tx, txi, extra)
    dpre, short_d, short_u = lax.optimization_barrier((dpre, short_d, short_u))
    got = exchange(flat(back))
    other_u = lax.ppermute(short_u, "batch", swap)
    other_d = lax.ppermute(short_d, "batch", swap)
    mapped = call(
        back_kernel, struct(PLANES, BF16), [HBM, VMEM], HBM,
        [held, held, sems, sems], 2 * 10**9, 2 * big, LIMIT, "point_map_back",
    )(dpre, point_weight)
    grad_spec = call(
        spec_kernel, struct((16, 2, C, 512), F32), [SMEM] + [VMEM] * 4, VMEM,
        [pltpu.VMEM((520, 128), F32), pltpu.VMEM((32, 512), F32)],
        10**7, 2 * MIB, 32, "spectral_gradient",
    )(which, modes_u, other_u, rows_d, other_d)
    input_grad, grad_point, grad_bias = call(
        final_kernel, (struct(GIVEN, BF16), struct((C, C), F32), struct((1, C), F32)),
        [VMEM, HBM, VMEM, VMEM], (HBM, VMEM, VMEM),
        [zf, pltpu.VMEM((3072 + 96, 128), F32), gather, planes, held, held, sems, sems],
        4 * 10**9, 2 * big, LIMIT, "input_gradient",
    )(got, mapped, tyt, zb)
    return input_grad, grad_spec, grad_point, grad_bias.reshape(C)


def solution(mesh):
    planes = P("batch", None, "slab", None, None)
    return jax.shard_map(
        body,
        mesh=mesh,
        in_specs=(planes, planes, P("slab", None, None, None), P(), P()),
        out_specs=(planes, P("slab", None, None, None), P(), P()),
        check_vma=False,
    )
```
